256 devices in a mesh: dp: 32 (over y, z), expert: 8 (over x, core).
Axes of the slice: x: 4, y: 4, z: 8, core: 2. Of those that a mesh axis runs over, the one named last changes fastest.
Arguments:
- residual: bfloat16 [32768, 3072], P(('dp', 'expert')), may hold values from -36 to 36
- context: bfloat16 [32768, 24, 128], P('dp', 'expert'), may hold values from -6 to 6
- master: float32 [24, 128, 3072], P('expert', 'dp'), may hold values from -0.109375 to 0.109375
- grad: float32 [24, 128, 3072], P('expert', 'dp'), may hold values from -6 to 6
- moment: float32 [24, 128, 3072], P('expert', 'dp'), may hold values from -1.8 to 1.8
- second: float32 [24, 128, 3072], P('expert', 'dp'), may hold values from 0.0005 to 0.02
- gain: float32 [3072], replicated, may hold values from 0.5 to 1.5
- token_ids: int32 [32768], P(('dp', 'expert')), may hold values from 0 to 51199
- table_one: int32 [51200], replicated, may hold values from 0 to 31
- table_two: int32 [51200], replicated, may hold values from 0 to 31
- w_in: bfloat16 [32, 1536, 5120], P('dp', None, 'expert'), may hold values from -0.15625 to 0.15625
- w_out: bfloat16 [32, 5120, 1536], P('dp', 'expert'), may hold values from -0.078125 to 0.078125
Outputs:
- mixed: bfloat16 [32768, 3072], P(('dp', 'expert'))
The draws below stay inside these ranges and needn't reach their ends.
All inputs are finite; a program needn't handle non-finite values.
Results may differ from the reference program's by a relative error of at most 0.009.
Values may be sent and summed in bfloat16 or wider, within the bound.
No kernel may reach another device: no remote copies, remote signals or barrier semaphores. Data moves between devices by JAX's collectives and lax.ppermute only.
A program may use at most 64 MiB of HBM per device.

```python
import math
import jax
import jax.numpy as jnp
import numpy as np
from jax import lax

D = 3072
DH = 1536
FF = 5120
HEADS = 24
HDIM = 128
VOCAB = 51200
TOK_DEV = 128
TOKENS = 32768
EXPERTS = 32
CAP = 5
N_EXPERT = 8


def draw_residual(key, part):
    value_key, row_key, column_key = jax.random.split(jax.random.fold_in(key, 17), 3)
    values = jax.random.truncated_normal(value_key, -4.0, 4.0, (TOKENS, D), jnp.float32)
    row_scale = jnp.exp(jax.random.uniform(row_key, (TOKENS, 1), jnp.float32, jnp.log(0.3), jnp.log(3.0)))
    column_scale = jnp.exp(jax.random.uniform(column_key, (1, D), jnp.float32, jnp.log(0.3), jnp.log(3.0)))
    return (values * row_scale * column_scale).astype(jnp.bfloat16)


def touch_ends(result, key, least, top_value):
    longest = result.shape.index(max(result.shape))
    spots = []
    for shift in (0, 1):
        where = [jax.random.randint(jax.random.fold_in(key, axis), (), 0, length) for axis, length in enumerate(result.shape)]
        where[longest] = (where[longest] + shift) % result.shape[longest]
        spots.append(tuple(where))
    return result.at[spots[0]].set(least).at[spots[1]].set(top_value)


def levels(rng, extent, cuts, low, largest):
    factor_of = 1.0
    for dim, parts in cuts:
        steps = jax.random.uniform(jax.random.fold_in(jax.random.fold_in(rng, 6), dim), (parts,), jnp.float32, low / len(cuts), largest / len(cuts))
        factor_of = factor_of * jnp.repeat(jnp.exp(steps), extent[dim] // parts).reshape((-1,) + (1,) * (len(extent) - 1 - dim))
    return factor_of


def rank_bounds(number_of, skew):
    portions = [(1 << 20) // math.isqrt(grade ** skew) + 1 for grade in range(1, number_of + 1)]
    scale = 1 + sum(portions) // (1 << 30)
    return np.cumsum(np.array([max(1, weight // scale) for weight in portions]))


def ranked_ids(key, extent, number_of, lean):
    grid = rank_bounds(number_of, lean)
    ticket = jax.random.randint(jax.random.fold_in(key, 1), extent, 0, int(grid[number_of - 1]))
    standing = jnp.searchsorted(jnp.asarray(grid, jnp.int32), ticket, side="right")
    return jax.random.permutation(jax.random.fold_in(key, 2), number_of)[standing].astype(jnp.int32)


def normal_values(key, shape, deviation, reach, cuts=(), held_as=jnp.bfloat16):
    drawn = jax.random.normal(key, shape, jnp.float32) * deviation
    if len(cuts) > 0:
        drawn = levels(key, shape, cuts, -0.22, 0.18) * drawn
    return jnp.clip(drawn, min=-reach, max=reach).astype(held_as)


def setup_inputs(seed: int = 0) -> dict:
    arg_keys = jax.random.split(jax.random.key(seed), 13)
    return {
        "residual": draw_residual(jax.random.fold_in(arg_keys[12], 71), 0),
        "context": normal_values(arg_keys[1], (TOKENS, HEADS, HDIM), 1.0, 6.0, ((0, 32), (1, 8))),
        "master": normal_values(arg_keys[2], (HEADS, HDIM, D), (HEADS * HDIM) ** -0.5, 0.109375, ((0, 8), (1, 32)), jnp.float32),
        "grad": normal_values(arg_keys[3], (HEADS, HDIM, D), 1.0, 6.0, ((0, 8), (1, 32)), jnp.float32),
        "moment": normal_values(arg_keys[4], (HEADS, HDIM, D), 0.3, 1.8, ((0, 8), (1, 32)), jnp.float32),
        "second": jnp.clip(jnp.exp(math.log(0.02) - 3.6888794 * jax.random.uniform(arg_keys[5], (HEADS, HDIM, D), jnp.float32) ** levels(arg_keys[5], (HEADS, HDIM, D), ((0, 8), (1, 32)), -0.2, 0.2)), 0.0005, 0.02),
        "gain": jnp.clip(1.0 + 0.1 * jax.random.normal(arg_keys[6], (D,), jnp.float32), 0.5, 1.5),
        "token_ids": touch_ends(ranked_ids(arg_keys[7], (TOKENS,), VOCAB, 2), jax.random.fold_in(arg_keys[7], 3), 0, VOCAB - 1).astype(jnp.int32),
        "table_one": touch_ends(jax.random.randint(arg_keys[8], (VOCAB,), 0, EXPERTS), jax.random.fold_in(arg_keys[8], 1), 0, EXPERTS - 1).astype(jnp.int32),
        "table_two": touch_ends(jax.random.randint(arg_keys[9], (VOCAB,), 0, EXPERTS), jax.random.fold_in(arg_keys[9], 1), 0, EXPERTS - 1).astype(jnp.int32),
        "w_in": normal_values(arg_keys[10], (EXPERTS, DH, FF), DH ** -0.5, 0.15625, ((0, 32), (2, 8))),
        "w_out": normal_values(arg_keys[11], (EXPERTS, FF, DH), FF ** -0.5, 0.078125, ((0, 32), (1, 8))),
    }


lr_rate = 0.01
beta_one = 0.9
beta_two = 0.999
adam_step = 10.0
eps_adam = 1e-08
eps_norm = 1e-05

def adam_weight(master, grad, moment, second):
    new_moment = beta_one * moment + (1.0 - beta_one) * grad
    new_second = beta_two * second + (1.0 - beta_two) * grad * grad
    corr_one = 1.0 - beta_one ** adam_step
    corr_two = 1.0 - beta_two ** adam_step
    update = new_moment / corr_one / (jnp.sqrt(new_second / corr_two) + eps_adam)
    return (master - lr_rate * update).astype(jnp.bfloat16)

def slot_tables(routes_of, experts, capacity):
    onehot = (routes_of[..., None] == jnp.arange(experts, dtype=jnp.int32)).astype(jnp.int32)
    before = jnp.cumsum(onehot, axis=-2) - onehot
    slot_rank = lax.optimization_barrier(jnp.sum(before * onehot, axis=-1))
    match_expert = routes_of[..., None, :] == jnp.arange(experts, dtype=jnp.int32)[:, None]
    match_slot = slot_rank[..., None, :] == jnp.arange(capacity, dtype=jnp.int32)[:, None]
    return (match_expert[..., :, None, :] & match_slot[..., None, :, :]).astype(jnp.bfloat16)

def reference(residual, context, master, grad, moment, second, gain, token_ids, table_one, table_two, w_in, w_out):
    weight = adam_weight(master, grad, moment, second)
    group_width = HEADS // N_EXPERT * HDIM
    ctx_groups = jnp.transpose(context.reshape(TOKENS, N_EXPERT, group_width), (1, 0, 2))
    weight_groups = weight.reshape(N_EXPERT, group_width, D)

    def add_group(running, inputs):
        term = jnp.dot(inputs[0], inputs[1], preferred_element_type=jnp.float32).astype(jnp.bfloat16)
        term = lax.optimization_barrier(term)
        return (running + term.astype(jnp.float32), None)
    attn, _ = lax.scan(add_group, jnp.zeros((TOKENS, D), jnp.float32), (ctx_groups, weight_groups))
    state = residual.astype(jnp.float32) + attn
    scale = lax.rsqrt(lax.optimization_barrier(jnp.mean(state * state, axis=-1, keepdims=True)) + eps_norm)
    normed = (state * scale * gain.astype(jnp.float32)).astype(jnp.bfloat16)
    blocks = TOKENS // TOK_DEV
    halves_wide = normed.reshape(blocks, TOK_DEV, 2, DH).astype(jnp.float32)
    routes = jnp.stack([table_one[token_ids], table_two[token_ids]]).reshape(2, blocks, TOK_DEV)
    dispatch = slot_tables(routes, EXPERTS, CAP)
    by_expert = jnp.transpose(dispatch, (2, 0, 1, 3, 4)).astype(jnp.float32)
    slice_width = FF // N_EXPERT

    def one_expert(running, inputs):
        table, weight_in, weight_out = inputs
        gathered = jnp.einsum('kbst,btkd->kbsd', table, halves_wide)
        rows_in = gathered.astype(jnp.bfloat16).reshape(-1, DH)
        inner = jnp.dot(rows_in, weight_in, preferred_element_type=jnp.float32)
        hidden = jax.nn.gelu(inner, approximate=True).astype(jnp.bfloat16)
        hidden_parts = hidden.reshape(-1, N_EXPERT, slice_width).astype(jnp.float32)
        out_parts = weight_out.reshape(N_EXPERT, slice_width, DH).astype(jnp.float32)
        pieces = jnp.einsum('rcf,cfd->crd', hidden_parts, out_parts).astype(jnp.bfloat16)
        pieces = lax.optimization_barrier(pieces)
        expert_out = lax.optimization_barrier(jnp.sum(pieces.astype(jnp.float32), axis=0)).astype(jnp.bfloat16)
        expert_out = lax.optimization_barrier(expert_out)
        expert_out = expert_out.astype(jnp.float32).reshape(2, blocks, CAP, DH)
        return (running + jnp.einsum('kbst,kbsd->btkd', table, expert_out), None)
    routed, _ = lax.scan(one_expert, jnp.zeros((blocks, TOK_DEV, 2, DH), jnp.float32), (by_expert, w_in, w_out))
    return (state + routed.reshape(TOKENS, D)).astype(jnp.bfloat16)
```

```python
import jax
import jax.numpy as jnp
from jax import lax
from jax.sharding import PartitionSpec as P

lr_rate = 0.01
beta_one = 0.9
beta_two = 0.999
adam_step = 10.0
eps_adam = 1e-08
eps_norm = 1e-05


def adam_weight(master, grad, moment, second):
    new_moment = beta_one * moment + (1.0 - beta_one) * grad
    new_second = beta_two * second + (1.0 - beta_two) * grad * grad
    corr_one = 1.0 - beta_one**adam_step
    corr_two = 1.0 - beta_two**adam_step
    update = new_moment / corr_one / (jnp.sqrt(new_second / corr_two) + eps_adam)
    return (master - lr_rate * update).astype(jnp.bfloat16)


def slot_tables(routes_of, experts, capacity):
    tokens = routes_of.shape[-1]
    same = routes_of[..., :, None] == routes_of[..., None, :]
    earlier = jnp.arange(tokens)[None, :] < jnp.arange(tokens)[:, None]
    slot_rank = jnp.sum((same & earlier).astype(jnp.int32), axis=-1)
    match_expert = routes_of[..., None, :] == jnp.arange(experts, dtype=jnp.int32)[:, None]
    match_slot = slot_rank[..., None, :] == jnp.arange(capacity, dtype=jnp.int32)[:, None]
    return (match_expert[..., :, None, :] & match_slot[..., None, :, :]).astype(jnp.bfloat16)


def on_device(
    residual,
    context,
    master,
    grad,
    moment,
    second,
    gain,
    token_ids,
    table_one,
    table_two,
    w_in,
    w_out,
):
    experts = lax.axis_size("dp") * w_in.shape[0]
    tok_count = residual.shape[0]
    model_width = residual.shape[1]
    half_width = model_width // 2
    capacity = max(2, 5 * tok_count // (4 * experts))
    fresh = adam_weight(master, grad, moment, second)
    weight_all = lax.all_gather(fresh, "dp", axis=1, tiled=True)
    weight_rows = weight_all.reshape(-1, model_width)
    ctx_rows = context.reshape(context.shape[0], -1)
    attn = lax.psum_scatter(
        jnp.dot(ctx_rows, weight_rows, preferred_element_type=jnp.float32).astype(jnp.bfloat16),
        "expert",
        scatter_dimension=0,
        tiled=True,
    ).astype(jnp.float32)
    state = residual.astype(jnp.float32) + attn
    scale = lax.rsqrt(jnp.mean(state * state, axis=-1, keepdims=True) + eps_norm)
    normed = (state * scale * gain).astype(jnp.bfloat16)
    halves = normed.reshape(tok_count, 2, half_width)
    routes = jnp.stack([table_one[token_ids], table_two[token_ids]])
    dispatch = slot_tables(routes, experts, capacity)
    outgoing = jnp.einsum(
        "kest,tkd->eksd", dispatch, halves, preferred_element_type=jnp.float32
    ).astype(jnp.bfloat16)
    arrived = lax.all_to_all(outgoing, "dp", split_axis=0, concat_axis=0, tiled=True)
    rows_here = arrived.reshape(-1, half_width)
    inner = jnp.dot(
        lax.all_gather(rows_here, "expert", axis=0, tiled=True),
        w_in[0],
        preferred_element_type=jnp.float32,
    )
    hidden = jax.nn.gelu(inner, approximate=True).astype(jnp.bfloat16)
    partial_rows = jnp.dot(hidden, w_out[0], preferred_element_type=jnp.float32)
    expert_out = lax.psum_scatter(
        partial_rows.astype(jnp.bfloat16), "expert", scatter_dimension=0, tiled=True
    )
    shaped = expert_out.reshape(experts, 2, capacity, half_width)
    returned = lax.all_to_all(shaped, "dp", split_axis=0, concat_axis=0, tiled=True)
    routed = jnp.einsum("kest,eksd->tkd", dispatch, returned, preferred_element_type=jnp.float32)
    routed = routed.reshape(tok_count, model_width)
    return (state + routed).astype(jnp.bfloat16)


def solution(mesh):
    return jax.shard_map(
        on_device,
        mesh=mesh,
        in_specs=(
            P(("dp", "expert"), None),
            P("dp", "expert", None),
            P("expert", "dp", None),
            P("expert", "dp", None),
            P("expert", "dp", None),
            P("expert", "dp", None),
            P(),
            P(("dp", "expert")),
            P(),
            P(),
            P("dp", None, "expert"),
            P("dp", "expert", None),
        ),
        out_specs=P(("dp", "expert"), None),
        check_vma=False,
    )
```

```python
import jax
import jax.numpy as jnp
from jax import lax
from jax.sharding import PartitionSpec as P

lr_rate = 0.01
beta_one = 0.9
beta_two = 0.999
adam_step = 10.0
eps_adam = 1e-08
eps_norm = 1e-05

CAP = 5
NX, NY, NZ = 4, 4, 8
F32 = jnp.float32
BF16 = jnp.bfloat16


def adam_weight(master, grad, moment, second):
    new_moment = beta_one * moment + (1.0 - beta_one) * grad
    new_second = beta_two * second + (1.0 - beta_two) * grad * grad
    corr_one = 1.0 - beta_one**adam_step
    corr_two = 1.0 - beta_two**adam_step
    update = new_moment / corr_one / (jnp.sqrt(new_second / corr_two) + eps_adam)
    return (master - lr_rate * update).astype(BF16)


def along_z(x, step):
    return lax.ppermute(
        x, "dp", [(NZ * y + z, NZ * y + (z + step) % NZ) for y in range(NY) for z in range(NZ)]
    )


def along_y(x, step):
    return lax.ppermute(
        x, "dp", [(NZ * y + z, NZ * ((y + step) % NY) + z) for y in range(NY) for z in range(NZ)]
    )


def along_x(x, step):
    return lax.ppermute(x, "expert", [(i, (i + 2 * step) % (2 * NX)) for i in range(2 * NX)])


def other_core(x):
    return lax.ppermute(x, "expert", [(i, i ^ 1) for i in range(2 * NX)])


def dot(a, b):
    return jnp.dot(a, b, preferred_element_type=F32)


def gather_ring4(x, shift):
    half = x.shape[0] // 2
    before, after = shift(x, 1), shift(x, -1)
    far_top, far_bottom = shift(before[:half], 1), shift(after[half:], -1)
    return before, after, far_top, far_bottom


def scatter_ring4(own, right, far, left):
    half = far.shape[0] // 2
    from_left, from_right = along_x(far[:half], 1), along_x(far[half:], -1)
    right = jnp.concatenate(
        [(right[:half].astype(F32) + from_left.astype(F32)).astype(BF16), right[half:].astype(BF16)]
    )
    left = jnp.concatenate(
        [left[:half].astype(BF16), (left[half:].astype(F32) + from_right.astype(F32)).astype(BF16)]
    )
    from_left, from_right = along_x(right, 1), along_x(left, -1)
    return own.astype(F32) + from_left.astype(F32) + from_right.astype(F32)


def expert_rows(rows, w_in, w_out, w_in_other, w_out_other):
    def half(x, w_a, w_b):
        hidden = jax.nn.gelu(dot(x, w_a), approximate=True).astype(BF16)
        return dot(hidden, w_b)

    def both(x):
        return (half(x, w_in, w_out) + half(x, w_in_other, w_out_other)).astype(BF16)

    width = w_in.shape[0]
    quarter = width // 4
    main = both(rows[:, :width])
    rest = both(rows[:, width:].reshape(-1, width))
    return jnp.concatenate([main, rest.reshape(-1, quarter)], axis=1)


def on_device(
    residual,
    context,
    master,
    grad,
    moment,
    second,
    gain,
    token_ids,
    table_one,
    table_two,
    w_in,
    w_out,
):
    tokens, width = residual.shape
    half_width = width // 2
    experts = NY * NZ
    place = lax.axis_index("expert")
    x_at, core = place // 2, place % 2
    dp_at = lax.axis_index("dp")
    y_at, z_at = dp_at // NZ, dp_at % NZ

    fresh = adam_weight(master, grad, moment, second)
    mid = width // 2
    up, down = along_z(fresh, 1), along_z(fresh, -1)
    blocks = [fresh, up, down]
    for _ in range(2):
        up, down = along_z(up, 1), along_z(down, -1)
        blocks += [up, down]
    far = jnp.concatenate([along_z(up[..., :mid], 1), along_z(down[..., mid:], -1)], axis=-1)
    blocks.append(far)
    z_shift = [0, -1, 1, -2, 2, -3, 3, 4]
    y_shift = [0, -1, 1, 2]
    rows_z = jnp.concatenate([b.reshape(-1, width) for b in blocks])
    parts = [rows_z, *gather_ring4(rows_z, along_y)]
    weight = jnp.concatenate(parts + [other_core(p) for p in parts])

    n_heads, head_rows = fresh.shape[:2]
    group = n_heads * head_rows * NY * NZ
    col = jnp.arange(group)
    per_z = n_heads * head_rows
    pick_z = (z_at + jnp.array(z_shift)[(col // per_z) % NZ]) % NZ
    pick_y = (y_at + jnp.array(y_shift)[col // (per_z * NZ)]) % NY
    head = (col // head_rows) % n_heads
    source = head * (head_rows * NY * NZ) + (pick_y * NZ + pick_z) * head_rows + col % head_rows
    order = (jnp.arange(group)[:, None] == source[None, :]).astype(BF16)
    ctx = context.reshape(NX, 2, tokens, group)
    ctx = lax.dynamic_index_in_dim(ctx, core, 1, False), lax.dynamic_index_in_dim(ctx, 1 - core, 1, False)
    ctx = [jnp.concatenate([lax.dynamic_index_in_dim(c, (x_at + s) % NX, 0, False) for s in (2, 1, 3, 0)]) for c in ctx]
    ctx = [dot(c, order).astype(BF16) for c in ctx]
    ctx = jnp.concatenate([ctx[0], other_core(ctx[1])], axis=1)

    w_in, w_out = w_in[0], w_out[0]
    w_in_other, w_out_other = other_core(w_in), other_core(w_out)

    far = dot(ctx[:tokens], weight).astype(BF16)
    near = dot(ctx[tokens:], weight)
    attn = scatter_ring4(near[2 * tokens :], near[:tokens], far, near[tokens : 2 * tokens])
    state = residual.astype(F32) + attn
    scale = lax.rsqrt(jnp.mean(state * state, axis=-1, keepdims=True) + eps_norm)
    normed = (state * scale * gain).astype(BF16)

    routes = jnp.stack([table_one[token_ids], table_two[token_ids]])
    same = routes[:, :, None] == routes[:, None, :]
    earlier = jnp.arange(tokens)[None, :] < jnp.arange(tokens)[:, None]
    rank = jnp.sum((same & earlier).astype(jnp.int32), axis=-1)
    slot = rank + CAP * jnp.arange(2)[:, None]
    main_at = jnp.where((rank < CAP) & (slot < 8), routes * 8 + slot, -1)
    rest_at = jnp.where((rank[1] < CAP) & (slot[1] >= 8), routes[1] * 8 + (slot[1] - 8) * 4, -8)
    line = jnp.arange(8 * experts)[:, None]
    to_main = (line == main_at.reshape(1, -1)).astype(BF16)
    quarter = half_width // 4
    rest_cols = jnp.concatenate([rest_at + q for q in range(4)])
    to_rest = (line == rest_cols[None, :]).astype(BF16)
    halves = jnp.concatenate([normed[:, :half_width], normed[:, half_width:]])
    quarters = jnp.concatenate(
        [normed[:, half_width + q * quarter : half_width + (q + 1) * quarter] for q in range(4)]
    )
    outgoing = jnp.concatenate([dot(to_main, halves), dot(to_rest, quarters)], axis=1).astype(BF16)

    arrived = lax.all_to_all(outgoing, "dp", split_axis=0, concat_axis=0, tiled=True)
    before, after, far_top, far_bottom = gather_ring4(arrived, along_x)
    weights = w_in, w_out, w_in_other, w_out_other
    own = expert_rows(arrived, *weights)
    left = expert_rows(before, *weights)
    right = expert_rows(after, *weights)
    far = expert_rows(jnp.concatenate([far_top, far_bottom]), *weights)
    sums = scatter_ring4(own, right, far, left).astype(BF16)
    returned = lax.all_to_all(sums, "dp", split_axis=0, concat_axis=0, tiled=True)

    from_main = lax.dot_general(
        to_main.reshape(-1, 2, tokens), returned[:, :half_width], (((0,), (0,)), ((), ())), preferred_element_type=F32
    )
    from_rest = lax.dot_general(
        to_rest.reshape(-1, 4, tokens), returned[:, half_width:], (((0,), (0,)), ((), ())), preferred_element_type=F32
    )
    second_half = from_main[1] + jnp.concatenate([from_rest[q] for q in range(4)], axis=1)
    routed = jnp.concatenate([from_main[0], second_half], axis=1)
    return (state + routed).astype(BF16)


def solution(mesh):
    return jax.shard_map(
        on_device,
        mesh=mesh,
        in_specs=(
            P(("dp", "expert"), None),
            P("dp", "expert", None),
            P("expert", "dp", None),
            P("expert", "dp", None),
            P("expert", "dp", None),
            P("expert", "dp", None),
            P(),
            P(("dp", "expert")),
            P(),
            P(),
            P("dp", None, "expert"),
            P("dp", "expert", None),
        ),
        out_specs=P(("dp", "expert"), None),
        check_vma=False,
    )
```

```python
import jax
import jax.numpy as jnp
from jax import lax
from jax.experimental import pallas as pl
from jax.experimental.pallas import tpu as pltpu
from jax.sharding import PartitionSpec as P

lr_rate = 0.01
beta_one = 0.9
beta_two = 0.999
adam_step = 10.0
eps_adam = 1e-08
eps_norm = 1e-05

CAP = 5
NX, NY, NZ = 4, 4, 8
F32 = jnp.float32
BF16 = jnp.bfloat16


def adam_weight(master, grad, moment, second):
    new_moment = beta_one * moment + (1.0 - beta_one) * grad
    new_second = beta_two * second + (1.0 - beta_two) * grad * grad
    corr_one = 1.0 - beta_one**adam_step
    corr_two = 1.0 - beta_two**adam_step
    update = new_moment / corr_one / (jnp.sqrt(new_second / corr_two) + eps_adam)
    return (master - lr_rate * update).astype(BF16)


def along_z(x, step):
    return lax.ppermute(
        x, "dp", [(NZ * y + z, NZ * y + (z + step) % NZ) for y in range(NY) for z in range(NZ)]
    )


def along_y(x, step):
    return lax.ppermute(
        x, "dp", [(NZ * y + z, NZ * ((y + step) % NY) + z) for y in range(NY) for z in range(NZ)]
    )


def along_x(x, step):
    return lax.ppermute(x, "expert", [(i, (i + 2 * step) % (2 * NX)) for i in range(2 * NX)])


def other_core(x):
    return lax.ppermute(x, "expert", [(i, i ^ 1) for i in range(2 * NX)])


def dot(a, b):
    return jnp.dot(a, b, preferred_element_type=F32)


def add(a, b):
    return (a.astype(F32) + b.astype(F32)).astype(BF16)


def gather_x(top, bottom):
    left_top, right_bottom = along_x(top, 1), along_x(bottom, -1)
    left_bottom, right_top = along_x(bottom, 1), along_x(top, -1)
    far_top, far_bottom = along_x(left_top, 1), along_x(right_bottom, -1)
    return (left_top, left_bottom), (right_top, right_bottom), (far_top, far_bottom)


def scatter_x(own, right, far, left):
    from_left, from_right = along_x(far[0], 1), along_x(far[1], -1)
    left_bottom, right_top = along_x(right[1], 1), along_x(left[0], -1)
    left_top = along_x(add(right[0], from_left), 1)
    right_bottom = along_x(add(left[1], from_right), -1)
    top = own[0].astype(F32) + left_top.astype(F32) + right_top.astype(F32)
    bottom = own[1].astype(F32) + left_bottom.astype(F32) + right_bottom.astype(F32)
    return jnp.concatenate([top, bottom])


def join_kernel(*refs):
    *blocks, far_a, far_b, out = refs
    heads, rows, width = blocks[0].shape
    pieces = [b[h].astype(F32) for b in blocks for h in range(heads)]
    for h in range(heads):
        pieces.append(jnp.concatenate([far_a[h].astype(F32), far_b[h].astype(F32)], axis=1))
    per = 16 // rows
    for i in range(len(pieces) // per):
        out[16 * i : 16 * (i + 1), :] = jnp.concatenate(pieces[per * i : per * (i + 1)], axis=0).astype(BF16)


def join_rows(blocks, far_a, far_b):
    heads, rows, width = blocks[0].shape
    n = (len(blocks) + 1) * heads * rows
    return pl.pallas_call(
        join_kernel,
        out_shape=jax.ShapeDtypeStruct((n, width), BF16),
        in_specs=[pl.BlockSpec(memory_space=pltpu.VMEM)] * (len(blocks) + 2),
        out_specs=pl.BlockSpec(memory_space=pltpu.VMEM),
        compiler_params=pltpu.CompilerParams(vmem_limit_bytes=16 << 20),
        cost_estimate=pl.CostEstimate(flops=0, bytes_accessed=4 * n * width, transcendentals=0),
    )(*blocks, far_a, far_b)


def expert_kernel(top, bottom, w_in, w_out, w_in_other, w_out_other, out_top, out_bottom, x, y):
    width = w_in.shape[0]
    quarter = width // 4
    n = top.shape[0]
    few = n // 4
    at = lax.broadcasted_iota(jnp.int32, (few, n), 0)
    line = lax.broadcasted_iota(jnp.int32, (few, n), 1)
    base = (at // 2) * 8 + (at % 2) * 4
    at_t = lax.broadcasted_iota(jnp.int32, (n, few), 1)
    line_t = lax.broadcasted_iota(jnp.int32, (n, few), 0)
    base_t = (at_t // 2) * 8 + (at_t % 2) * 4
    for i, half in enumerate((top, bottom)):
        x[n * i : n * (i + 1), :] = half[:, :width]
        for q in range(4):
            pick = (line == base + q).astype(F32).astype(BF16)
            x[2 * n + few * i : 2 * n + few * (i + 1), quarter * q : quarter * (q + 1)] = dot(pick, half[:, width:]).astype(BF16)
    hidden = jax.nn.gelu(dot(x[...], w_in[...]), approximate=True).astype(BF16)
    hidden_other = jax.nn.gelu(dot(x[...], w_in_other[...]), approximate=True).astype(BF16)
    y[...] = (dot(hidden, w_out[...]) + dot(hidden_other, w_out_other[...])).astype(BF16)
    for i, half in enumerate((out_top, out_bottom)):
        half[:, :width] = y[n * i : n * (i + 1), :]
        total = 0.0
        for q in range(4):
            put = (line_t == base_t + q).astype(F32).astype(BF16)
            total += dot(put, y[2 * n + few * i : 2 * n + few * (i + 1), quarter * q : quarter * (q + 1)])
        half[:, width:] = total.astype(BF16)


def expert_rows(halves, w_in, w_out, w_in_other, w_out_other):
    n, cols = halves[0].shape
    width, hidden = w_in.shape
    vmem = pl.BlockSpec(memory_space=pltpu.VMEM)
    return pl.pallas_call(
        expert_kernel,
        out_shape=[jax.ShapeDtypeStruct((n, cols), BF16)] * 2,
        in_specs=[vmem] * 6,
        out_specs=[vmem] * 2,
        scratch_shapes=[pltpu.VMEM((n * 5 // 2, width), BF16)] * 2,
        compiler_params=pltpu.CompilerParams(vmem_limit_bytes=32 << 20),
        cost_estimate=pl.CostEstimate(
            flops=n * 5 * width * hidden * 4, bytes_accessed=8 * width * hidden + 8 * n * cols, transcendentals=n * 5 * hidden
        ),
    )(*halves, w_in, w_out, w_in_other, w_out_other)


def on_device(
    residual,
    context,
    master,
    grad,
    moment,
    second,
    gain,
    token_ids,
    table_one,
    table_two,
    w_in,
    w_out,
):
    tokens, width = residual.shape
    half_width = width // 2
    experts = NY * NZ
    place = lax.axis_index("expert")
    x_at, core = place // 2, place % 2
    dp_at = lax.axis_index("dp")
    y_at, z_at = dp_at // NZ, dp_at % NZ

    fresh = adam_weight(master, grad, moment, second)
    mid = width // 2
    up, down = along_z(fresh, 1), along_z(fresh, -1)
    blocks = [fresh, up, down]
    for _ in range(2):
        up, down = along_z(up, 1), along_z(down, -1)
        blocks += [up, down]
    far_a, far_b = along_z(up[..., :mid], 1), along_z(down[..., mid:], -1)
    w_in, w_out = w_in[0], w_out[0]
    w_in_other, w_out_other = other_core(w_in), other_core(w_out)
    far_a, w_in_other, w_out_other = lax.optimization_barrier((far_a, w_in_other, w_out_other))
    rows_z = join_rows(blocks, far_a, far_b)
    z_shift = [0, -1, 1, -2, 2, -3, 3, 4]
    y_shift = [0, -1, 1, 2]
    half_z = rows_z.shape[0] // 2
    before, after = along_y(rows_z, 1), along_y(rows_z, -1)
    far_a, far_b = along_y(before[:half_z], 1), along_y(after[half_z:], -1)
    parts = [rows_z, before, after, far_a, far_b]
    weight = jnp.concatenate(parts + [other_core(p) for p in parts])

    n_heads, head_rows = fresh.shape[:2]
    group = n_heads * head_rows * NY * NZ
    col = jnp.arange(group)
    per_z = n_heads * head_rows
    pick_z = (z_at + jnp.array(z_shift)[(col // per_z) % NZ]) % NZ
    pick_y = (y_at + jnp.array(y_shift)[col // (per_z * NZ)]) % NY
    head = (col // head_rows) % n_heads
    source = head * (head_rows * NY * NZ) + (pick_y * NZ + pick_z) * head_rows + col % head_rows
    order = (jnp.arange(group)[:, None] == source[None, :]).astype(BF16)
    ctx = context.reshape(NX, 2, tokens, group)
    ctx = lax.dynamic_index_in_dim(ctx, core, 1, False), lax.dynamic_index_in_dim(ctx, 1 - core, 1, False)
    ctx = [jnp.concatenate([lax.dynamic_index_in_dim(c, (x_at + s) % NX, 0, False) for s in (2, 1, 3, 0)]) for c in ctx]
    ctx = [dot(c, order).astype(BF16) for c in ctx]
    ctx = jnp.concatenate([ctx[0], other_core(ctx[1])], axis=1)

    half = tokens // 2
    far = dot(ctx[:tokens], weight).astype(BF16)
    near = dot(ctx[tokens:], weight).astype(BF16)
    near = [(near[i * tokens : i * tokens + half], near[i * tokens + half : (i + 1) * tokens]) for i in range(3)]
    attn = scatter_x(near[2], near[0], (far[:half], far[half:]), near[1])
    state = residual.astype(F32) + attn
    scale = lax.rsqrt(jnp.mean(state * state, axis=-1, keepdims=True) + eps_norm)
    normed = (state * scale * gain).astype(BF16)

    routes = jnp.stack([table_one[token_ids], table_two[token_ids]])
    same = routes[:, :, None] == routes[:, None, :]
    earlier = jnp.arange(tokens)[None, :] < jnp.arange(tokens)[:, None]
    rank = jnp.sum((same & earlier).astype(jnp.int32), axis=-1)
    slot = rank + CAP * jnp.arange(2)[:, None]
    main_at = jnp.where((rank < CAP) & (slot < 8), routes * 8 + slot, -1)
    rest_at = jnp.where((rank[1] < CAP) & (slot[1] >= 8), routes[1] * 8 + (slot[1] - 8) * 4, -8)
    line = jnp.arange(8 * experts)[:, None]
    to_main = (line == main_at.reshape(1, -1)).astype(BF16)
    quarter = half_width // 4
    rest_cols = jnp.concatenate([rest_at + q for q in range(4)])
    to_rest = (line == rest_cols[None, :]).astype(BF16)
    halves = jnp.concatenate([normed[:, :half_width], normed[:, half_width:]])
    quarters = jnp.concatenate(
        [normed[:, half_width + q * quarter : half_width + (q + 1) * quarter] for q in range(4)]
    )
    outgoing = jnp.concatenate([dot(to_main, halves), dot(to_rest, quarters)], axis=1).astype(BF16)

    arrived = lax.all_to_all(outgoing, "dp", split_axis=0, concat_axis=0, tiled=True)
    n = arrived.shape[0] // 2
    held = arrived[:n], arrived[n:]
    left, right, far = gather_x(*held)
    weights = w_in, w_out, w_in_other, w_out_other
    own, left, right, far = [expert_rows(h, *weights) for h in (held, left, right, far)]
    sums = scatter_x(own, right, far, left).astype(BF16)
    returned = lax.all_to_all(sums, "dp", split_axis=0, concat_axis=0, tiled=True)

    from_main = lax.dot_general(
        to_main.reshape(-1, 2, tokens), returned[:, :half_width], (((0,), (0,)), ((), ())), preferred_element_type=F32
    )
    from_rest = lax.dot_general(
        to_rest.reshape(-1, 4, tokens), returned[:, half_width:], (((0,), (0,)), ((), ())), preferred_element_type=F32
    )
    second_half = from_main[1] + jnp.concatenate([from_rest[q] for q in range(4)], axis=1)
    routed = jnp.concatenate([from_main[0], second_half], axis=1)
    return (state + routed).astype(BF16)


def solution(mesh):
    return jax.shard_map(
        on_device,
        mesh=mesh,
        in_specs=(
            P(("dp", "expert"), None),
            P("dp", "expert", None),
            P("expert", "dp", None),
            P("expert", "dp", None),
            P("expert", "dp", None),
            P("expert", "dp", None),
            P(),
            P(("dp", "expert")),
            P(),
            P(),
            P("dp", None, "expert"),
            P("dp", "expert", None),
        ),
        out_specs=P(("dp", "expert"), None),
        check_vma=False,
    )
```

```python
import jax
import jax.numpy as jnp
from jax import lax
from jax.experimental import pallas as pl
from jax.experimental.pallas import tpu as pltpu
from jax.sharding import PartitionSpec as P

lr_rate = 0.01
beta_one = 0.9
beta_two = 0.999
adam_step = 10.0
eps_adam = 1e-08
eps_norm = 1e-05

CAP = 5
NX, NY, NZ = 4, 4, 8
F32 = jnp.float32
BF16 = jnp.bfloat16


def adam_weight(master, grad, moment, second):
    new_moment = beta_one * moment + (1.0 - beta_one) * grad
    new_second = beta_two * second + (1.0 - beta_two) * grad * grad
    corr_one = 1.0 - beta_one**adam_step
    corr_two = 1.0 - beta_two**adam_step
    update = new_moment / corr_one / (jnp.sqrt(new_second / corr_two) + eps_adam)
    return (master - lr_rate * update).astype(BF16)


def along_z(x, step):
    return lax.ppermute(
        x, "dp", [(NZ * y + z, NZ * y + (z + step) % NZ) for y in range(NY) for z in range(NZ)]
    )


def along_y(x, step):
    return lax.ppermute(
        x, "dp", [(NZ * y + z, NZ * ((y + step) % NY) + z) for y in range(NY) for z in range(NZ)]
    )


def along_x(x, step):
    return lax.ppermute(x, "expert", [(i, (i + 2 * step) % (2 * NX)) for i in range(2 * NX)])


def other_core(x):
    return lax.ppermute(x, "expert", [(i, i ^ 1) for i in range(2 * NX)])


def dot(a, b):
    return jnp.dot(a, b, preferred_element_type=F32)


def add(a, b):
    return (a.astype(F32) + b.astype(F32)).astype(BF16)


def gather_x(top, bottom):
    left_top, right_bottom = along_x(top, 1), along_x(bottom, -1)
    left_bottom, right_top = along_x(bottom, 1), along_x(top, -1)
    far_top, far_bottom = along_x(left_top, 1), along_x(right_bottom, -1)
    return (left_top, left_bottom), (right_top, right_bottom), (far_top, far_bottom)


def scatter_x(own, right, far, left):
    from_left, from_right = along_x(far[0], 1), along_x(far[1], -1)
    left_bottom, right_top = along_x(right[1], 1), along_x(left[0], -1)
    left_top = along_x(add(right[0], from_left), 1)
    right_bottom = along_x(add(left[1], from_right), -1)
    top = own[0].astype(F32) + left_top.astype(F32) + right_top.astype(F32)
    bottom = own[1].astype(F32) + left_bottom.astype(F32) + right_bottom.astype(F32)
    return jnp.concatenate([top, bottom])


VMEM = pl.BlockSpec(memory_space=pltpu.VMEM)
SMEM = pl.BlockSpec(memory_space=pltpu.SMEM)


def join_kernel(*refs):
    *blocks, far_a, far_b, out_a, out_b = refs
    heads, rows, width = blocks[0].shape
    pieces = [b[h].astype(F32) for b in blocks for h in range(heads)]
    for h in range(heads):
        pieces.append(jnp.concatenate([far_a[h].astype(F32), far_b[h].astype(F32)], axis=1))
    per = 16 // rows
    for i in range(len(pieces) // per):
        sixteen = jnp.concatenate(pieces[per * i : per * (i + 1)], axis=0).astype(BF16)
        out_a[16 * i : 16 * (i + 1), :] = sixteen[:, : width // 2]
        out_b[16 * i : 16 * (i + 1), :] = sixteen[:, width // 2 :]


def join_rows(blocks, far_a, far_b):
    heads, rows, width = blocks[0].shape
    n = (len(blocks) + 1) * heads * rows
    return pl.pallas_call(
        join_kernel,
        out_shape=[jax.ShapeDtypeStruct((n, width // 2), BF16)] * 2,
        in_specs=[VMEM] * (len(blocks) + 2),
        out_specs=[VMEM] * 2,
        compiler_params=pltpu.CompilerParams(vmem_limit_bytes=16 << 20),
        cost_estimate=pl.CostEstimate(flops=0, bytes_accessed=4 * n * width, transcendentals=0),
    )(*blocks, far_a, far_b)


def context_kernel(starts, context, source, out):
    heads, _, size = context.shape
    group = source.shape[1]
    line = lax.broadcasted_iota(jnp.int32, (size, group), 0)
    order = [(line + size * h == source[...]).astype(F32).astype(BF16) for h in range(heads)]
    rows = out.shape[0] // starts.shape[0]
    for i in range(starts.shape[0]):
        at = pl.ds(pl.multiple_of(starts[i], rows), rows)
        out[rows * i : rows * (i + 1), :] = sum(dot(context[h, at, :], order[h]) for h in range(heads)).astype(BF16)


def arrange_context(starts, context, source):
    heads, tokens, size = context.shape
    return pl.pallas_call(
        context_kernel,
        out_shape=jax.ShapeDtypeStruct((tokens, heads * size), BF16),
        in_specs=[SMEM, VMEM, VMEM],
        out_specs=VMEM,
        compiler_params=pltpu.CompilerParams(vmem_limit_bytes=16 << 20),
        cost_estimate=pl.CostEstimate(
            flops=2 * tokens * heads * size * heads * size, bytes_accessed=4 * tokens * heads * size, transcendentals=0
        ),
    )(starts, context, source)


def project_kernel(ctx, *refs):
    *parts, mine, other, weight = refs
    n = parts[0].shape[0]
    for i, part in enumerate(parts):
        weight[n * i : n * (i + 1), :] = part[...]
    half = ctx.shape[0] // 2
    step = 512
    for i in range(weight.shape[1] // step):
        cols = slice(step * i, step * (i + 1))
        mine[:, cols] = dot(ctx[:half, :], weight[:, cols]).astype(BF16)
        other[:, cols] = dot(ctx[half:, :], weight[:, cols]).astype(BF16)


def project(ctx, parts):
    tokens, group = ctx.shape
    cols = parts[0].shape[1]
    return pl.pallas_call(
        project_kernel,
        out_shape=[jax.ShapeDtypeStruct((tokens // 2, cols), BF16)] * 2,
        in_specs=[VMEM] * (1 + len(parts)),
        out_specs=[VMEM] * 2,
        scratch_shapes=[pltpu.VMEM((group, cols), BF16)],
        compiler_params=pltpu.CompilerParams(vmem_limit_bytes=24 << 20),
        cost_estimate=pl.CostEstimate(
            flops=2 * tokens * group * cols, bytes_accessed=2 * (tokens * group + group * cols + tokens * cols), transcendentals=0
        ),
    )(ctx, *parts)


def expert_kernel(top, bottom, w_in, w_out, w_in_other, w_out_other, out_top, out_bottom, x, y):
    width = w_in.shape[0]
    quarter = width // 4
    n = top.shape[0]
    few = n // 4
    at = lax.broadcasted_iota(jnp.int32, (few, n), 0)
    line = lax.broadcasted_iota(jnp.int32, (few, n), 1)
    base = (at // 2) * 8 + (at % 2) * 4
    at_t = lax.broadcasted_iota(jnp.int32, (n, few), 1)
    line_t = lax.broadcasted_iota(jnp.int32, (n, few), 0)
    base_t = (at_t // 2) * 8 + (at_t % 2) * 4
    for i, half in enumerate((top, bottom)):
        x[n * i : n * (i + 1), :] = half[:, :width]
        for q in range(4):
            pick = (line == base + q).astype(F32).astype(BF16)
            x[2 * n + few * i : 2 * n + few * (i + 1), quarter * q : quarter * (q + 1)] = dot(pick, half[:, width:]).astype(BF16)
    hidden = jax.nn.gelu(dot(x[...], w_in[...]), approximate=True).astype(BF16)
    hidden_other = jax.nn.gelu(dot(x[...], w_in_other[...]), approximate=True).astype(BF16)
    y[...] = (dot(hidden, w_out[...]) + dot(hidden_other, w_out_other[...])).astype(BF16)
    for i, half in enumerate((out_top, out_bottom)):
        half[:, :width] = y[n * i : n * (i + 1), :]
        total = 0.0
        for q in range(4):
            put = (line_t == base_t + q).astype(F32).astype(BF16)
            total += dot(put, y[2 * n + few * i : 2 * n + few * (i + 1), quarter * q : quarter * (q + 1)])
        half[:, width:] = total.astype(BF16)


def expert_rows(halves, w_in, w_out, w_in_other, w_out_other):
    n, cols = halves[0].shape
    width, hidden = w_in.shape
    return pl.pallas_call(
        expert_kernel,
        out_shape=[jax.ShapeDtypeStruct((n, cols), BF16)] * 2,
        in_specs=[VMEM] * 6,
        out_specs=[VMEM] * 2,
        scratch_shapes=[pltpu.VMEM((n * 5 // 2, width), BF16)] * 2,
        compiler_params=pltpu.CompilerParams(vmem_limit_bytes=32 << 20),
        cost_estimate=pl.CostEstimate(
            flops=n * 5 * width * hidden * 4, bytes_accessed=8 * width * hidden + 8 * n * cols, transcendentals=n * 5 * hidden
        ),
    )(*halves, w_in, w_out, w_in_other, w_out_other)


def on_device(
    residual,
    context,
    master,
    grad,
    moment,
    second,
    gain,
    token_ids,
    table_one,
    table_two,
    w_in,
    w_out,
):
    tokens, width = residual.shape
    half_width = width // 2
    experts = NY * NZ
    place = lax.axis_index("expert")
    x_at, core = place // 2, place % 2
    dp_at = lax.axis_index("dp")
    y_at, z_at = dp_at // NZ, dp_at % NZ

    fresh = adam_weight(master, grad, moment, second)
    mid = width // 2
    up, down = along_z(fresh, 1), along_z(fresh, -1)
    blocks = [fresh, up, down]
    for _ in range(2):
        up, down = along_z(up, 1), along_z(down, -1)
        blocks += [up, down]
    far_a, far_b = along_z(up[..., :mid], 1), along_z(down[..., mid:], -1)
    w_in, w_out = w_in[0], w_out[0]
    w_in_other, w_out_other = other_core(w_in), other_core(w_out)
    far_a, w_in_other, w_out_other = lax.optimization_barrier((far_a, w_in_other, w_out_other))
    rows_a, rows_b = join_rows(blocks, far_a, far_b)
    z_shift = [0, -1, 1, -2, 2, -3, 3, 4]
    y_shift = [0, -1, 1, 2]

    n_heads, head_rows = fresh.shape[:2]
    group = n_heads * head_rows * NY * NZ
    col = jnp.arange(group)
    per_z = n_heads * head_rows
    pick_z = (z_at + jnp.array(z_shift)[(col // per_z) % NZ]) % NZ
    pick_y = (y_at + jnp.array(y_shift)[col // (per_z * NZ)]) % NY
    head = (col // head_rows) % n_heads
    source = head * (head_rows * NY * NZ) + (pick_y * NZ + pick_z) * head_rows + col % head_rows
    starts = [(((x_at + s) % NX) * 2 + c) * tokens for c in (core, 1 - core) for s in (2, 1, 3, 0)]
    starts = jnp.stack(starts).astype(jnp.int32)
    rows_a, rows_b, context = lax.optimization_barrier((rows_a, rows_b, context))
    ctx = arrange_context(starts, jnp.transpose(context, (1, 0, 2)), source[None, :].astype(jnp.int32))

    attn = []
    for rows, way in ((rows_a, 1), (rows_b, -1)):
        before, after = along_y(rows, 1), along_y(rows, -1)
        far = along_y(before if way == 1 else after, way)
        mine, other = project(ctx, [rows, before, after, far])
        other = other_core(other)
        far, right, left, own = [
            mine[i * tokens : (i + 1) * tokens].astype(F32) + other[i * tokens : (i + 1) * tokens].astype(F32) for i in range(4)
        ]
        passed = along_x(far.astype(BF16), way).astype(F32)
        right, left = (right + passed, left) if way == 1 else (right, left + passed)
        attn.append(own + along_x(right.astype(BF16), 1).astype(F32) + along_x(left.astype(BF16), -1).astype(F32))
    attn = jnp.concatenate(attn, axis=1)
    state = residual.astype(F32) + attn
    scale = lax.rsqrt(jnp.mean(state * state, axis=-1, keepdims=True) + eps_norm)
    normed = (state * scale * gain).astype(BF16)

    routes = jnp.stack([table_one[token_ids], table_two[token_ids]])
    same = routes[:, :, None] == routes[:, None, :]
    earlier = jnp.arange(tokens)[None, :] < jnp.arange(tokens)[:, None]
    rank = jnp.sum((same & earlier).astype(jnp.int32), axis=-1)
    slot = rank + CAP * jnp.arange(2)[:, None]
    main_at = jnp.where((rank < CAP) & (slot < 8), routes * 8 + slot, -1)
    rest_at = jnp.where((rank[1] < CAP) & (slot[1] >= 8), routes[1] * 8 + (slot[1] - 8) * 4, -8)
    line = jnp.arange(8 * experts)[:, None]
    to_main = (line == main_at.reshape(1, -1)).astype(BF16)
    quarter = half_width // 4
    rest_cols = jnp.concatenate([rest_at + q for q in range(4)])
    to_rest = (line == rest_cols[None, :]).astype(BF16)
    halves = jnp.concatenate([normed[:, :half_width], normed[:, half_width:]])
    quarters = jnp.concatenate(
        [normed[:, half_width + q * quarter : half_width + (q + 1) * quarter] for q in range(4)]
    )
    outgoing = jnp.concatenate([dot(to_main, halves), dot(to_rest, quarters)], axis=1).astype(BF16)

    arrived = lax.all_to_all(outgoing, "dp", split_axis=0, concat_axis=0, tiled=True)
    n = arrived.shape[0] // 2
    held = arrived[:n], arrived[n:]
    left, right, far = gather_x(*held)
    weights = w_in, w_out, w_in_other, w_out_other
    own, left, right, far = [expert_rows(h, *weights) for h in (held, left, right, far)]
    sums = scatter_x(own, right, far, left).astype(BF16)
    returned = lax.all_to_all(sums, "dp", split_axis=0, concat_axis=0, tiled=True)

    from_main = lax.dot_general(
        to_main.reshape(-1, 2, tokens), returned[:, :half_width], (((0,), (0,)), ((), ())), preferred_element_type=F32
    )
    from_rest = lax.dot_general(
        to_rest.reshape(-1, 4, tokens), returned[:, half_width:], (((0,), (0,)), ((), ())), preferred_element_type=F32
    )
    second_half = from_main[1] + jnp.concatenate([from_rest[q] for q in range(4)], axis=1)
    routed = jnp.concatenate([from_main[0], second_half], axis=1)
    return (state + routed).astype(BF16)


def solution(mesh):
    return jax.shard_map(
        on_device,
        mesh=mesh,
        in_specs=(
            P(("dp", "expert"), None),
            P("dp", "expert", None),
            P("expert", "dp", None),
            P("expert", "dp", None),
            P("expert", "dp", None),
            P("expert", "dp", None),
            P(),
            P(("dp", "expert")),
            P(),
            P(),
            P("dp", None, "expert"),
            P("dp", "expert", None),
        ),
        out_specs=P(("dp", "expert"), None),
        check_vma=False,
    )
```

```python
import jax
import jax.numpy as jnp
from jax import lax
from jax.experimental import pallas as pl
from jax.experimental.pallas import tpu as pltpu
from jax.sharding import PartitionSpec as P

lr_rate = 0.01
beta_one = 0.9
beta_two = 0.999
adam_step = 10.0
eps_adam = 1e-08
eps_norm = 1e-05

CAP = 5
NX, NY, NZ = 4, 4, 8
F32 = jnp.float32
BF16 = jnp.bfloat16


def adam_weight(master, grad, moment, second):
    new_moment = beta_one * moment + (1.0 - beta_one) * grad
    new_second = beta_two * second + (1.0 - beta_two) * grad * grad
    corr_one = 1.0 - beta_one**adam_step
    corr_two = 1.0 - beta_two**adam_step
    update = new_moment / corr_one / (jnp.sqrt(new_second / corr_two) + eps_adam)
    return (master - lr_rate * update).astype(BF16)


def along_z(x, step):
    return lax.ppermute(
        x, "dp", [(NZ * y + z, NZ * y + (z + step) % NZ) for y in range(NY) for z in range(NZ)]
    )


def along_y(x, step):
    return lax.ppermute(
        x, "dp", [(NZ * y + z, NZ * ((y + step) % NY) + z) for y in range(NY) for z in range(NZ)]
    )


def along_x(x, step):
    return lax.ppermute(x, "expert", [(i, (i + 2 * step) % (2 * NX)) for i in range(2 * NX)])


def other_core(x):
    return lax.ppermute(x, "expert", [(i, i ^ 1) for i in range(2 * NX)])


def dot(a, b):
    return jnp.dot(a, b, preferred_element_type=F32)


def scatter_x(own, right, far, left, way):
    passed = along_x(far.astype(BF16), way).astype(F32)
    right, left = (right + passed, left) if way == 1 else (right, left + passed)
    return own + along_x(right.astype(BF16), 1).astype(F32) + along_x(left.astype(BF16), -1).astype(F32)


VMEM = pl.BlockSpec(memory_space=pltpu.VMEM)
SMEM = pl.BlockSpec(memory_space=pltpu.SMEM)


def join_kernel(*refs):
    *blocks, far_a, far_b, out_a, out_b = refs
    heads, rows, width = blocks[0].shape
    pieces = [b[h].astype(F32) for b in blocks for h in range(heads)]
    for h in range(heads):
        pieces.append(jnp.concatenate([far_a[h].astype(F32), far_b[h].astype(F32)], axis=1))
    per = 16 // rows
    for i in range(len(pieces) // per):
        sixteen = jnp.concatenate(pieces[per * i : per * (i + 1)], axis=0).astype(BF16)
        out_a[16 * i : 16 * (i + 1), :] = sixteen[:, : width // 2]
        out_b[16 * i : 16 * (i + 1), :] = sixteen[:, width // 2 :]


def join_rows(blocks, far_a, far_b):
    heads, rows, width = blocks[0].shape
    n = (len(blocks) + 1) * heads * rows
    return pl.pallas_call(
        join_kernel,
        out_shape=[jax.ShapeDtypeStruct((n, width // 2), BF16)] * 2,
        in_specs=[VMEM] * (len(blocks) + 2),
        out_specs=[VMEM] * 2,
        compiler_params=pltpu.CompilerParams(vmem_limit_bytes=16 << 20),
        cost_estimate=pl.CostEstimate(flops=0, bytes_accessed=4 * n * width, transcendentals=0),
    )(*blocks, far_a, far_b)


def context_kernel(starts, context, source, out):
    heads, _, size = context.shape
    group = source.shape[1]
    line = lax.broadcasted_iota(jnp.int32, (size, group), 0)
    order = [(line + size * h == source[...]).astype(F32).astype(BF16) for h in range(heads)]
    rows = out.shape[0] // starts.shape[0]
    for i in range(starts.shape[0]):
        at = pl.ds(pl.multiple_of(starts[i], rows), rows)
        out[rows * i : rows * (i + 1), :] = sum(dot(context[h, at, :], order[h]) for h in range(heads)).astype(BF16)


def arrange_context(starts, context, source):
    heads, tokens, size = context.shape
    return pl.pallas_call(
        context_kernel,
        out_shape=jax.ShapeDtypeStruct((tokens, heads * size), BF16),
        in_specs=[SMEM, VMEM, VMEM],
        out_specs=VMEM,
        compiler_params=pltpu.CompilerParams(vmem_limit_bytes=16 << 20),
        cost_estimate=pl.CostEstimate(
            flops=2 * tokens * heads * size * heads * size, bytes_accessed=4 * tokens * heads * size, transcendentals=0
        ),
    )(starts, context, source)


def project_kernel(ctx, *refs):
    *parts, mine, other, weight = refs
    n = parts[0].shape[0]
    for i, part in enumerate(parts):
        weight[n * i : n * (i + 1), :] = part[...]
    half = ctx.shape[0] // 2
    step = 512
    for i in range(weight.shape[1] // step):
        cols = slice(step * i, step * (i + 1))
        mine[:, cols] = dot(ctx[:half, :], weight[:, cols]).astype(BF16)
        other[:, cols] = dot(ctx[half:, :], weight[:, cols]).astype(BF16)


def project(ctx, parts):
    tokens, group = ctx.shape
    cols = parts[0].shape[1]
    return pl.pallas_call(
        project_kernel,
        out_shape=[jax.ShapeDtypeStruct((tokens // 2, cols), BF16)] * 2,
        in_specs=[VMEM] * (1 + len(parts)),
        out_specs=[VMEM] * 2,
        scratch_shapes=[pltpu.VMEM((group, cols), BF16)],
        compiler_params=pltpu.CompilerParams(vmem_limit_bytes=24 << 20),
        cost_estimate=pl.CostEstimate(flops=1000, bytes_accessed=1000, transcendentals=0),
    )(ctx, *parts)


def expert_kernel(rows, w_in, w_out, w_in_other, w_out_other, out, x, y):
    width = w_in.shape[0]
    quarter = width // 4
    n = rows.shape[0]
    few = n // 4
    at = lax.broadcasted_iota(jnp.int32, (few, n), 0)
    line = lax.broadcasted_iota(jnp.int32, (few, n), 1)
    at_t = lax.broadcasted_iota(jnp.int32, (n, few), 1)
    line_t = lax.broadcasted_iota(jnp.int32, (n, few), 0)
    x[:n, :] = rows[:, :width]
    for q in range(4):
        pick = (line == 4 * at + q).astype(F32).astype(BF16)
        x[n:, quarter * q : quarter * (q + 1)] = dot(pick, rows[:, width:]).astype(BF16)
    hidden = jax.nn.gelu(dot(x[...], w_in[...]), approximate=True).astype(BF16)
    hidden_other = jax.nn.gelu(dot(x[...], w_in_other[...]), approximate=True).astype(BF16)
    y[...] = (dot(hidden, w_out[...]) + dot(hidden_other, w_out_other[...])).astype(BF16)
    out[:, :width] = y[:n, :]
    total = 0.0
    for q in range(4):
        put = (line_t == 4 * at_t + q).astype(F32).astype(BF16)
        total += dot(put, y[n:, quarter * q : quarter * (q + 1)])
    out[:, width:] = total.astype(BF16)


def expert_rows(rows, w_in, w_out, w_in_other, w_out_other):
    n, cols = rows.shape
    width, hidden = w_in.shape
    return pl.pallas_call(
        expert_kernel,
        out_shape=jax.ShapeDtypeStruct((n, cols), BF16),
        in_specs=[VMEM] * 5,
        out_specs=VMEM,
        scratch_shapes=[pltpu.VMEM((n * 5 // 4, width), BF16)] * 2,
        compiler_params=pltpu.CompilerParams(vmem_limit_bytes=32 << 20),
        cost_estimate=pl.CostEstimate(flops=1000, bytes_accessed=1000, transcendentals=0),
    )(rows, w_in, w_out, w_in_other, w_out_other)


def on_device(
    residual,
    context,
    master,
    grad,
    moment,
    second,
    gain,
    token_ids,
    table_one,
    table_two,
    w_in,
    w_out,
):
    tokens, width = residual.shape
    half_width = width // 2
    experts = NY * NZ
    place = lax.axis_index("expert")
    x_at, core = place // 2, place % 2
    dp_at = lax.axis_index("dp")
    y_at, z_at = dp_at // NZ, dp_at % NZ

    fresh = adam_weight(master, grad, moment, second)
    mid = width // 2
    up, down = along_z(fresh, 1), along_z(fresh, -1)
    blocks = [fresh, up, down]
    for _ in range(2):
        up, down = along_z(up, 1), along_z(down, -1)
        blocks += [up, down]
    far_a, far_b = along_z(up[..., :mid], 1), along_z(down[..., mid:], -1)
    w_in, w_out = w_in[0], w_out[0]
    w_in_other, w_out_other = other_core(w_in), other_core(w_out)
    rows_a, rows_b = join_rows(blocks, far_a, far_b)
    z_shift = [0, -1, 1, -2, 2, -3, 3, 4]
    y_shift = [0, -1, 1, 2]

    n_heads, head_rows = fresh.shape[:2]
    group = n_heads * head_rows * NY * NZ
    col = jnp.arange(group)
    per_z = n_heads * head_rows
    pick_z = (z_at + jnp.array(z_shift)[(col // per_z) % NZ]) % NZ
    pick_y = (y_at + jnp.array(y_shift)[col // (per_z * NZ)]) % NY
    head = (col // head_rows) % n_heads
    source = head * (head_rows * NY * NZ) + (pick_y * NZ + pick_z) * head_rows + col % head_rows
    starts = [(((x_at + s) % NX) * 2 + c) * tokens for c in (core, 1 - core) for s in (2, 1, 3, 0)]
    starts = jnp.stack(starts).astype(jnp.int32)
    rows_a, rows_b, context = lax.optimization_barrier((rows_a, rows_b, context))
    ctx = arrange_context(starts, jnp.transpose(context, (1, 0, 2)), source[None, :].astype(jnp.int32))

    before_a, after_a = along_y(rows_a, 1), along_y(rows_a, -1)
    far_a = along_y(before_a, 1)
    rows_b, after_a = lax.optimization_barrier((rows_b, after_a))
    after_b = along_y(rows_b, -1)
    rows_b, far_a, after_b, w_in_other, w_out_other = lax.optimization_barrier(
        (rows_b, far_a, after_b, w_in_other, w_out_other)
    )
    before_b = along_y(rows_b, 1)
    far_b = along_y(after_b, -1)

    def blocks_of(products):
        mine, other = [p.astype(F32).reshape(4, tokens, -1) for p in products]
        return [mine[i] + other[i] for i in range(4)]

    mine, other = project(ctx, [rows_a, before_a, after_a, far_a])
    far, right_a, left, own_a = blocks_of((mine, other_core(other)))
    before_b, far = lax.optimization_barrier((before_b, far.astype(BF16)))
    passed, left_a = lax.optimization_barrier((along_x(far, 1), along_x(left.astype(BF16), -1)))
    right_a = (right_a + passed.astype(F32)).astype(BF16)
    mine, other = project(ctx, [rows_b, before_b, after_b, far_b])
    token_ids, other = lax.optimization_barrier((token_ids, other_core(other)))
    far, right_b, left, own_b = blocks_of((mine, other))
    right_a, far = lax.optimization_barrier((right_a, far.astype(BF16)))
    right_a, passed = along_x(right_a, 1), along_x(far, -1)
    right_b = along_x(right_b.astype(BF16), 1)
    left_b = along_x((left + passed.astype(F32)).astype(BF16), -1)
    attn = [own_a + right_a.astype(F32) + left_a.astype(F32), own_b + right_b.astype(F32) + left_b.astype(F32)]
    attn = jnp.concatenate(attn, axis=1)
    state = residual.astype(F32) + attn
    scale = lax.rsqrt(jnp.mean(state * state, axis=-1, keepdims=True) + eps_norm)
    normed = (state * scale * gain).astype(BF16)

    routes = jnp.stack([table_one[token_ids], table_two[token_ids]])
    same = routes[:, :, None] == routes[:, None, :]
    earlier = jnp.arange(tokens)[None, :] < jnp.arange(tokens)[:, None]
    rank = jnp.sum((same & earlier).astype(jnp.int32), axis=-1)
    lines = CAP - 1
    main_at = jnp.where(rank < lines, routes * lines + rank, -1)
    rest_at = jnp.where(rank == lines, routes * lines, -lines)
    line = jnp.arange(lines * experts)[:, None]
    quarter = half_width // lines
    weights = w_in, w_out, w_in_other, w_out_other

    sent = []
    for k in range(2):
        half = normed[:, k * half_width : (k + 1) * half_width]
        quarters = jnp.concatenate([half[:, q * quarter : (q + 1) * quarter] for q in range(lines)])
        to_main = (line == main_at[k][None, :]).astype(BF16)
        to_rest = (line == jnp.concatenate([rest_at[k] + q for q in range(lines)])[None, :]).astype(BF16)
        rows = jnp.concatenate([dot(to_main, half), dot(to_rest, quarters)], axis=1).astype(BF16)
        rows = lax.all_to_all(rows.reshape(experts, lines, -1), "dp", split_axis=0, concat_axis=0, tiled=True)
        sent.append((to_main, to_rest, rows.reshape(experts * lines, -1)))

    mixed = []
    held_a, held_b = sent[0][2], sent[1][2]
    left_a, right_a = lax.optimization_barrier((along_x(held_a, 1), along_x(held_a, -1)))
    far_a = along_x(left_a, 1)
    held_b, far_a = lax.optimization_barrier((held_b, far_a))
    left_b, right_b = lax.optimization_barrier((along_x(held_b, 1), along_x(held_b, -1)))
    far_b = along_x(right_b, -1)
    gathered = (held_a, right_a, far_a, left_a), (held_b, right_b, far_b, left_b)
    for k, way in ((0, 1), (1, -1)):
        to_main, to_rest, _ = sent[k]
        blocks = [expert_rows(h, *weights).astype(F32) for h in gathered[k]]
        sums = scatter_x(*blocks, way).astype(BF16)
        back = lax.all_to_all(sums.reshape(experts, lines, -1), "dp", split_axis=0, concat_axis=0, tiled=True)
        back = back.reshape(experts * lines, -1)
        over = (((0,), (0,)), ((), ()))
        from_main = lax.dot_general(to_main, back[:, :half_width], over, preferred_element_type=F32)
        from_rest = lax.dot_general(to_rest, back[:, half_width:], over, preferred_element_type=F32)
        from_rest = jnp.concatenate([from_rest[q * tokens : (q + 1) * tokens] for q in range(lines)], axis=1)
        mixed.append((state[:, k * half_width : (k + 1) * half_width] + (from_main + from_rest)).astype(BF16))
    return jnp.concatenate(mixed, axis=1)


def solution(mesh):
    return jax.shard_map(
        on_device,
        mesh=mesh,
        in_specs=(
            P(("dp", "expert"), None),
            P("dp", "expert", None),
            P("expert", "dp", None),
            P("expert", "dp", None),
            P("expert", "dp", None),
            P("expert", "dp", None),
            P(),
            P(("dp", "expert")),
            P(),
            P(),
            P("dp", None, "expert"),
            P("dp", "expert", None),
        ),
        out_specs=P(("dp", "expert"), None),
        check_vma=False,
    )
```

```python
import jax
import jax.numpy as jnp
from jax import lax
from jax.experimental import pallas as pl
from jax.experimental.pallas import tpu as pltpu
from jax.sharding import PartitionSpec as P

lr_rate = 0.01
beta_one = 0.9
beta_two = 0.999
adam_step = 10.0
eps_adam = 1e-08
eps_norm = 1e-05

CAP = 5
NX, NY, NZ = 4, 4, 8
F32 = jnp.float32
BF16 = jnp.bfloat16


def adam_weight(master, grad, moment, second):
    new_moment = beta_one * moment + (1.0 - beta_one) * grad
    new_second = beta_two * second + (1.0 - beta_two) * grad * grad
    corr_one = 1.0 - beta_one**adam_step
    corr_two = 1.0 - beta_two**adam_step
    update = new_moment / corr_one / (jnp.sqrt(new_second / corr_two) + eps_adam)
    return (master - lr_rate * update).astype(BF16)


def along_z(x, step):
    return lax.ppermute(
        x, "dp", [(NZ * y + z, NZ * y + (z + step) % NZ) for y in range(NY) for z in range(NZ)]
    )


def along_y(x, step):
    return lax.ppermute(
        x, "dp", [(NZ * y + z, NZ * ((y + step) % NY) + z) for y in range(NY) for z in range(NZ)]
    )


def along_x(x, step):
    return lax.ppermute(x, "expert", [(i, (i + 2 * step) % (2 * NX)) for i in range(2 * NX)])


def other_core(x):
    return lax.ppermute(x, "expert", [(i, i ^ 1) for i in range(2 * NX)])


def dot(a, b):
    return jnp.dot(a, b, preferred_element_type=F32)


def add(a, b):
    return (a.astype(F32) + b.astype(F32)).astype(BF16)


def gather_x(top, bottom):
    left_top, right_bottom = along_x(top, 1), along_x(bottom, -1)
    left_bottom, right_top = along_x(bottom, 1), along_x(top, -1)
    far_top, far_bottom = along_x(left_top, 1), along_x(right_bottom, -1)
    return (left_top, left_bottom), (right_top, right_bottom), (far_top, far_bottom)


def scatter_x(own, right, far, left):
    from_left, from_right = lax.optimization_barrier((along_x(far[0], 1), along_x(far[1], -1)))
    left_bottom, right_top = along_x(right[1], 1), along_x(left[0], -1)
    left_top = along_x(add(right[0], from_left), 1)
    right_bottom = along_x(add(left[1], from_right), -1)
    top = own[0].astype(F32) + left_top.astype(F32) + right_top.astype(F32)
    bottom = own[1].astype(F32) + left_bottom.astype(F32) + right_bottom.astype(F32)
    return jnp.concatenate([top, bottom])


VMEM = pl.BlockSpec(memory_space=pltpu.VMEM)
SMEM = pl.BlockSpec(memory_space=pltpu.SMEM)


def join_kernel(*refs):
    *blocks, far_a, far_b, out_a, out_b = refs
    heads, rows, width = blocks[0].shape
    pieces = [b[h].astype(F32) for b in blocks for h in range(heads)]
    for h in range(heads):
        pieces.append(jnp.concatenate([far_a[h].astype(F32), far_b[h].astype(F32)], axis=1))
    per = 16 // rows
    for i in range(len(pieces) // per):
        sixteen = jnp.concatenate(pieces[per * i : per * (i + 1)], axis=0).astype(BF16)
        out_a[16 * i : 16 * (i + 1), :] = sixteen[:, : width // 2]
        out_b[16 * i : 16 * (i + 1), :] = sixteen[:, width // 2 :]


def join_rows(blocks, far_a, far_b):
    heads, rows, width = blocks[0].shape
    n = (len(blocks) + 1) * heads * rows
    return pl.pallas_call(
        join_kernel,
        out_shape=[jax.ShapeDtypeStruct((n, width // 2), BF16)] * 2,
        in_specs=[VMEM] * (len(blocks) + 2),
        out_specs=[VMEM] * 2,
        compiler_params=pltpu.CompilerParams(vmem_limit_bytes=16 << 20),
        cost_estimate=pl.CostEstimate(flops=0, bytes_accessed=4 * n * width, transcendentals=0),
    )(*blocks, far_a, far_b)


def context_kernel(starts, context, source, out):
    heads, _, size = context.shape
    group = source.shape[1]
    line = lax.broadcasted_iota(jnp.int32, (size, group), 0)
    order = [(line + size * h == source[...]).astype(F32).astype(BF16) for h in range(heads)]
    rows = out.shape[0] // starts.shape[0]
    for i in range(starts.shape[0]):
        at = pl.ds(pl.multiple_of(starts[i], rows), rows)
        out[rows * i : rows * (i + 1), :] = sum(dot(context[h, at, :], order[h]) for h in range(heads)).astype(BF16)


def arrange_context(starts, context, source):
    heads, tokens, size = context.shape
    return pl.pallas_call(
        context_kernel,
        out_shape=jax.ShapeDtypeStruct((tokens, heads * size), BF16),
        in_specs=[SMEM, VMEM, VMEM],
        out_specs=VMEM,
        compiler_params=pltpu.CompilerParams(vmem_limit_bytes=16 << 20),
        cost_estimate=pl.CostEstimate(
            flops=2 * tokens * heads * size * heads * size, bytes_accessed=4 * tokens * heads * size, transcendentals=0
        ),
    )(starts, context, source)


def project_kernel(ctx, *refs):
    *parts, mine, other, weight = refs
    n = parts[0].shape[0]
    for i, part in enumerate(parts):
        weight[n * i : n * (i + 1), :] = part[...]
    half = ctx.shape[0] // 2
    step = 512
    for i in range(weight.shape[1] // step):
        cols = slice(step * i, step * (i + 1))
        mine[:, cols] = dot(ctx[:half, :], weight[:, cols]).astype(BF16)
        other[:, cols] = dot(ctx[half:, :], weight[:, cols]).astype(BF16)


def project(ctx, parts):
    tokens, group = ctx.shape
    cols = parts[0].shape[1]
    return pl.pallas_call(
        project_kernel,
        out_shape=[jax.ShapeDtypeStruct((tokens // 2, cols), BF16)] * 2,
        in_specs=[VMEM] * (1 + len(parts)),
        out_specs=[VMEM] * 2,
        scratch_shapes=[pltpu.VMEM((group, cols), BF16)],
        compiler_params=pltpu.CompilerParams(vmem_limit_bytes=24 << 20),
        cost_estimate=pl.CostEstimate(
            flops=2 * tokens * group * cols, bytes_accessed=2 * (tokens * group + group * cols + tokens * cols), transcendentals=0
        ),
    )(ctx, *parts)


def expert_kernel(top, bottom, w_in, w_out, w_in_other, w_out_other, out_top, out_bottom, x, y):
    width = w_in.shape[0]
    quarter = width // 4
    n = top.shape[0]
    few = n // 4
    at = lax.broadcasted_iota(jnp.int32, (few, n), 0)
    line = lax.broadcasted_iota(jnp.int32, (few, n), 1)
    base = (at // 2) * 8 + (at % 2) * 4
    at_t = lax.broadcasted_iota(jnp.int32, (n, few), 1)
    line_t = lax.broadcasted_iota(jnp.int32, (n, few), 0)
    base_t = (at_t // 2) * 8 + (at_t % 2) * 4
    for i, half in enumerate((top, bottom)):
        x[n * i : n * (i + 1), :] = half[:, :width]
        for q in range(4):
            pick = (line == base + q).astype(F32).astype(BF16)
            x[2 * n + few * i : 2 * n + few * (i + 1), quarter * q : quarter * (q + 1)] = dot(pick, half[:, width:]).astype(BF16)
    hidden = jax.nn.gelu(dot(x[...], w_in[...]), approximate=True).astype(BF16)
    hidden_other = jax.nn.gelu(dot(x[...], w_in_other[...]), approximate=True).astype(BF16)
    y[...] = (dot(hidden, w_out[...]) + dot(hidden_other, w_out_other[...])).astype(BF16)
    for i, half in enumerate((out_top, out_bottom)):
        half[:, :width] = y[n * i : n * (i + 1), :]
        total = 0.0
        for q in range(4):
            put = (line_t == base_t + q).astype(F32).astype(BF16)
            total += dot(put, y[2 * n + few * i : 2 * n + few * (i + 1), quarter * q : quarter * (q + 1)])
        half[:, width:] = total.astype(BF16)


def expert_rows(halves, w_in, w_out, w_in_other, w_out_other):
    n, cols = halves[0].shape
    width, hidden = w_in.shape
    return pl.pallas_call(
        expert_kernel,
        out_shape=[jax.ShapeDtypeStruct((n, cols), BF16)] * 2,
        in_specs=[VMEM] * 6,
        out_specs=[VMEM] * 2,
        scratch_shapes=[pltpu.VMEM((n * 5 // 2, width), BF16)] * 2,
        compiler_params=pltpu.CompilerParams(vmem_limit_bytes=32 << 20),
        cost_estimate=pl.CostEstimate(flops=1000, bytes_accessed=1000, transcendentals=0),
    )(*halves, w_in, w_out, w_in_other, w_out_other)


def on_device(
    residual,
    context,
    master,
    grad,
    moment,
    second,
    gain,
    token_ids,
    table_one,
    table_two,
    w_in,
    w_out,
):
    tokens, width = residual.shape
    half_width = width // 2
    experts = NY * NZ
    place = lax.axis_index("expert")
    x_at, core = place // 2, place % 2
    dp_at = lax.axis_index("dp")
    y_at, z_at = dp_at // NZ, dp_at % NZ

    fresh = adam_weight(master, grad, moment, second)
    mid = width // 2
    up, down = along_z(fresh, 1), along_z(fresh, -1)
    blocks = [fresh, up, down]
    for _ in range(2):
        up, down = along_z(up, 1), along_z(down, -1)
        blocks += [up, down]
    far_a, far_b = along_z(up[..., :mid], 1), along_z(down[..., mid:], -1)
    w_in, w_out = w_in[0], w_out[0]
    w_in_other, w_out_other = other_core(w_in), other_core(w_out)
    rows_a, rows_b = join_rows(blocks, far_a, far_b)
    z_shift = [0, -1, 1, -2, 2, -3, 3, 4]
    y_shift = [0, -1, 1, 2]

    n_heads, head_rows = fresh.shape[:2]
    group = n_heads * head_rows * NY * NZ
    col = jnp.arange(group)
    per_z = n_heads * head_rows
    pick_z = (z_at + jnp.array(z_shift)[(col // per_z) % NZ]) % NZ
    pick_y = (y_at + jnp.array(y_shift)[col // (per_z * NZ)]) % NY
    head = (col // head_rows) % n_heads
    source = head * (head_rows * NY * NZ) + (pick_y * NZ + pick_z) * head_rows + col % head_rows
    starts = [(((x_at + s) % NX) * 2 + c) * tokens for c in (core, 1 - core) for s in (2, 1, 3, 0)]
    starts = jnp.stack(starts).astype(jnp.int32)
    rows_a, rows_b, context = lax.optimization_barrier((rows_a, rows_b, context))
    ctx = arrange_context(starts, jnp.transpose(context, (1, 0, 2)), source[None, :].astype(jnp.int32))

    before_a, after_a, before_b, after_b = along_y(rows_a, 1), along_y(rows_a, -1), along_y(rows_b, 1), along_y(rows_b, -1)
    before_a, after_b = lax.optimization_barrier((before_a, after_b))
    far_a, far_b = along_y(before_a, 1), along_y(after_b, -1)
    after_a, before_b, far_a, far_b, w_in_other, w_out_other = lax.optimization_barrier(
        (after_a, before_b, far_a, far_b, w_in_other, w_out_other)
    )

    def blocks_of(products):
        mine, other = [[p[i * tokens : (i + 1) * tokens].astype(F32) for i in range(4)] for p in products]
        return [a + b for a, b in zip(mine, other)]

    mine_a, other_a = project(ctx, [rows_a, before_a, after_a, far_a])
    mine_b, other_b = project(ctx, [rows_b, before_b, after_b, far_b])
    other_a, other_b = other_core(other_a), other_core(other_b)
    token_ids, other_b = lax.optimization_barrier((token_ids, other_b))
    far, right_a, left, own_a = blocks_of((mine_a, other_a))
    far, left = lax.optimization_barrier((far.astype(BF16), left.astype(BF16)))
    passed_a, left_a = along_x(far, 1), along_x(left, -1)
    far, right, left_b, own_b = blocks_of((mine_b, other_b))
    far, right = lax.optimization_barrier((far.astype(BF16), right.astype(BF16)))
    passed_b, right_b = along_x(far, -1), along_x(right, 1)
    right_a = along_x((right_a + passed_a.astype(F32)).astype(BF16), 1)
    left_b = along_x((left_b + passed_b.astype(F32)).astype(BF16), -1)
    attn = [own_a + right_a.astype(F32) + left_a.astype(F32), own_b + right_b.astype(F32) + left_b.astype(F32)]
    attn = jnp.concatenate(attn, axis=1)
    state = residual.astype(F32) + attn
    scale = lax.rsqrt(jnp.mean(state * state, axis=-1, keepdims=True) + eps_norm)
    normed = (state * scale * gain).astype(BF16)

    routes = jnp.stack([table_one[token_ids], table_two[token_ids]])
    same = routes[:, :, None] == routes[:, None, :]
    earlier = jnp.arange(tokens)[None, :] < jnp.arange(tokens)[:, None]
    rank = jnp.sum((same & earlier).astype(jnp.int32), axis=-1)
    slot = rank + CAP * jnp.arange(2)[:, None]
    main_at = jnp.where((rank < CAP) & (slot < 8), routes * 8 + slot, -1)
    rest_at = jnp.where((rank[1] < CAP) & (slot[1] >= 8), routes[1] * 8 + (slot[1] - 8) * 4, -8)
    line = jnp.arange(8 * experts)[:, None]
    to_main = (line == main_at.reshape(1, -1)).astype(BF16)
    quarter = half_width // 4
    rest_cols = jnp.concatenate([rest_at + q for q in range(4)])
    to_rest = (line == rest_cols[None, :]).astype(BF16)
    halves = jnp.concatenate([normed[:, :half_width], normed[:, half_width:]])
    quarters = jnp.concatenate(
        [normed[:, half_width + q * quarter : half_width + (q + 1) * quarter] for q in range(4)]
    )
    outgoing = jnp.concatenate([dot(to_main, halves), dot(to_rest, quarters)], axis=1).astype(BF16)

    arrived = lax.all_to_all(outgoing, "dp", split_axis=0, concat_axis=0, tiled=True)
    n = arrived.shape[0] // 2
    held = arrived[:n], arrived[n:]
    left, right, far = gather_x(*held)
    weights = w_in, w_out, w_in_other, w_out_other
    own, left, right, far = [expert_rows(h, *weights) for h in (held, left, right, far)]
    sums = scatter_x(own, right, far, left).astype(BF16)
    returned = lax.all_to_all(sums, "dp", split_axis=0, concat_axis=0, tiled=True)

    from_main = lax.dot_general(
        to_main.reshape(-1, 2, tokens), returned[:, :half_width], (((0,), (0,)), ((), ())), preferred_element_type=F32
    )
    from_rest = lax.dot_general(
        to_rest.reshape(-1, 4, tokens), returned[:, half_width:], (((0,), (0,)), ((), ())), preferred_element_type=F32
    )
    second_half = from_main[1] + jnp.concatenate([from_rest[q] for q in range(4)], axis=1)
    routed = jnp.concatenate([from_main[0], second_half], axis=1)
    return (state + routed).astype(BF16)


def solution(mesh):
    return jax.shard_map(
        on_device,
        mesh=mesh,
        in_specs=(
            P(("dp", "expert"), None),
            P("dp", "expert", None),
            P("expert", "dp", None),
            P("expert", "dp", None),
            P("expert", "dp", None),
            P("expert", "dp", None),
            P(),
            P(("dp", "expert")),
            P(),
            P(),
            P("dp", None, "expert"),
            P("dp", "expert", None),
        ),
        out_specs=P(("dp", "expert"), None),
        check_vma=False,
    )
```

```python
import jax
import jax.numpy as jnp
from jax import lax
from jax.experimental import pallas as pl
from jax.experimental.pallas import tpu as pltpu
from jax.sharding import PartitionSpec as P

lr_rate = 0.01
beta_one = 0.9
beta_two = 0.999
adam_step = 10.0
eps_adam = 1e-08
eps_norm = 1e-05

CAP = 5
NX, NY, NZ = 4, 4, 8
F32 = jnp.float32
BF16 = jnp.bfloat16


def adam_weight(master, grad, moment, second):
    new_moment = beta_one * moment + (1.0 - beta_one) * grad
    new_second = beta_two * second + (1.0 - beta_two) * grad * grad
    corr_one = 1.0 - beta_one**adam_step
    corr_two = 1.0 - beta_two**adam_step
    update = new_moment / corr_one / (jnp.sqrt(new_second / corr_two) + eps_adam)
    return (master - lr_rate * update).astype(BF16)


def gather_z(x):
    groups = [[NZ * y + z for z in range(NZ)] for y in range(NY)]
    copies = jnp.broadcast_to(x[None], (NZ, *x.shape))
    return lax.all_to_all(copies, "dp", 0, 0, axis_index_groups=groups, tiled=True)


def along_y(x, step):
    return lax.ppermute(
        x, "dp", [(NZ * y + z, NZ * ((y + step) % NY) + z) for y in range(NY) for z in range(NZ)]
    )


def along_x(x, step):
    return lax.ppermute(x, "expert", [(i, (i + 2 * step) % (2 * NX)) for i in range(2 * NX)])


def other_core(x):
    return lax.ppermute(x, "expert", [(i, i ^ 1) for i in range(2 * NX)])


def dot(a, b):
    return jnp.dot(a, b, preferred_element_type=F32)


def add(a, b):
    return (a.astype(F32) + b.astype(F32)).astype(BF16)


def gather_x(top, bottom):
    left_top, right_bottom = along_x(top, 1), along_x(bottom, -1)
    left_bottom, right_top = along_x(bottom, 1), along_x(top, -1)
    far_top, far_bottom = along_x(left_top, 1), along_x(right_bottom, -1)
    return (left_top, left_bottom), (right_top, right_bottom), (far_top, far_bottom)


def scatter_x(own, right, far, left):
    from_left, from_right = lax.optimization_barrier((along_x(far[0], 1), along_x(far[1], -1)))
    left_bottom, right_top = along_x(right[1], 1), along_x(left[0], -1)
    left_top = along_x(add(right[0], from_left), 1)
    right_bottom = along_x(add(left[1], from_right), -1)
    top = own[0].astype(F32) + left_top.astype(F32) + right_top.astype(F32)
    bottom = own[1].astype(F32) + left_bottom.astype(F32) + right_bottom.astype(F32)
    return jnp.concatenate([top, bottom])


VMEM = pl.BlockSpec(memory_space=pltpu.VMEM)
SMEM = pl.BlockSpec(memory_space=pltpu.SMEM)


def join_kernel(blocks, out_a, out_b):
    n, heads, rows, width = blocks.shape
    per = 16 // rows
    for i in range(n * heads // per):
        pieces = [blocks[j // heads, j % heads].astype(F32) for j in range(per * i, per * (i + 1))]
        sixteen = jnp.concatenate(pieces, axis=0).astype(BF16)
        out_a[16 * i : 16 * (i + 1), :] = sixteen[:, : width // 2]
        out_b[16 * i : 16 * (i + 1), :] = sixteen[:, width // 2 :]


def join_rows(blocks):
    n, heads, rows, width = blocks.shape
    lines = n * heads * rows
    return pl.pallas_call(
        join_kernel,
        out_shape=[jax.ShapeDtypeStruct((lines, width // 2), BF16)] * 2,
        in_specs=[VMEM],
        out_specs=[VMEM] * 2,
        compiler_params=pltpu.CompilerParams(vmem_limit_bytes=12 << 20),
        cost_estimate=pl.CostEstimate(flops=0, bytes_accessed=4 * lines * width, transcendentals=0),
    )(blocks)


def context_kernel(starts, context, source, out):
    heads, _, size = context.shape
    group = source.shape[1]
    line = lax.broadcasted_iota(jnp.int32, (size, group), 0)
    order = [(line + size * h == source[...]).astype(F32).astype(BF16) for h in range(heads)]
    rows = out.shape[0] // starts.shape[0]
    for i in range(starts.shape[0]):
        at = pl.ds(pl.multiple_of(starts[i], rows), rows)
        out[rows * i : rows * (i + 1), :] = sum(dot(context[h, at, :], order[h]) for h in range(heads)).astype(BF16)


def arrange_context(starts, context, source):
    heads, tokens, size = context.shape
    return pl.pallas_call(
        context_kernel,
        out_shape=jax.ShapeDtypeStruct((tokens, heads * size), BF16),
        in_specs=[SMEM, VMEM, VMEM],
        out_specs=VMEM,
        compiler_params=pltpu.CompilerParams(vmem_limit_bytes=16 << 20),
        cost_estimate=pl.CostEstimate(
            flops=2 * tokens * heads * size * heads * size, bytes_accessed=4 * tokens * heads * size, transcendentals=0
        ),
    )(starts, context, source)


def project_kernel(ctx, *refs):
    *parts, mine, other, weight = refs
    n = parts[0].shape[0]
    for i, part in enumerate(parts):
        weight[n * i : n * (i + 1), :] = part[...]
    half = ctx.shape[0] // 2
    step = 512
    for i in range(weight.shape[1] // step):
        cols = slice(step * i, step * (i + 1))
        mine[:, cols] = dot(ctx[:half, :], weight[:, cols]).astype(BF16)
        other[:, cols] = dot(ctx[half:, :], weight[:, cols]).astype(BF16)


def project(ctx, parts):
    tokens, group = ctx.shape
    cols = parts[0].shape[1]
    return pl.pallas_call(
        project_kernel,
        out_shape=[jax.ShapeDtypeStruct((tokens // 2, cols), BF16)] * 2,
        in_specs=[VMEM] * (1 + len(parts)),
        out_specs=[VMEM] * 2,
        scratch_shapes=[pltpu.VMEM((group, cols), BF16)],
        compiler_params=pltpu.CompilerParams(vmem_limit_bytes=24 << 20),
        cost_estimate=pl.CostEstimate(
            flops=2 * tokens * group * cols, bytes_accessed=2 * (tokens * group + group * cols + tokens * cols), transcendentals=0
        ),
    )(ctx, *parts)


def expert_kernel(top, bottom, w_in, w_out, out_top, out_bottom, x, y):
    width = w_in.shape[0]
    quarter = width // 4
    n = top.shape[0]
    few = n // 4
    at = lax.broadcasted_iota(jnp.int32, (few, n), 0)
    line = lax.broadcasted_iota(jnp.int32, (few, n), 1)
    base = (at // 2) * 8 + (at % 2) * 4
    at_t = lax.broadcasted_iota(jnp.int32, (n, few), 1)
    line_t = lax.broadcasted_iota(jnp.int32, (n, few), 0)
    base_t = (at_t // 2) * 8 + (at_t % 2) * 4
    for i, half in enumerate((top, bottom)):
        x[n * i : n * (i + 1), :] = half[:, :width]
        for q in range(4):
            pick = (line == base + q).astype(F32).astype(BF16)
            x[2 * n + few * i : 2 * n + few * (i + 1), quarter * q : quarter * (q + 1)] = dot(pick, half[:, width:]).astype(BF16)
    hidden = jax.nn.gelu(dot(x[...], w_in[...]), approximate=True).astype(BF16)
    y[...] = dot(hidden, w_out[...]).astype(BF16)
    for i, half in enumerate((out_top, out_bottom)):
        half[:, :width] = y[n * i : n * (i + 1), :]
        total = 0.0
        for q in range(4):
            put = (line_t == base_t + q).astype(F32).astype(BF16)
            total += dot(put, y[2 * n + few * i : 2 * n + few * (i + 1), quarter * q : quarter * (q + 1)])
        half[:, width:] = total.astype(BF16)


def expert_rows(halves, w_in, w_out):
    n, cols = halves[0].shape
    width = w_in.shape[0]
    return pl.pallas_call(
        expert_kernel,
        out_shape=[jax.ShapeDtypeStruct((n, cols), BF16)] * 2,
        in_specs=[VMEM] * 4,
        out_specs=[VMEM] * 2,
        scratch_shapes=[pltpu.VMEM((n * 5 // 2, width), BF16)] * 2,
        compiler_params=pltpu.CompilerParams(vmem_limit_bytes=24 << 20),
        cost_estimate=pl.CostEstimate(flops=1000, bytes_accessed=1000, transcendentals=0),
    )(*halves, w_in, w_out)


def on_device(
    residual,
    context,
    master,
    grad,
    moment,
    second,
    gain,
    token_ids,
    table_one,
    table_two,
    w_in,
    w_out,
):
    tokens, width = residual.shape
    half_width = width // 2
    experts = NY * NZ
    place = lax.axis_index("expert")
    x_at, core = place // 2, place % 2
    dp_at = lax.axis_index("dp")
    y_at = dp_at // NZ

    fresh = adam_weight(master, grad, moment, second)
    w_in, w_out = w_in[0], w_out[0]
    w_in_other, w_out_other = other_core(w_in), other_core(w_out)
    rows_a, rows_b = join_rows(gather_z(fresh))
    y_shift = [0, -1, 1, 2]

    n_heads, head_rows = fresh.shape[:2]
    group = n_heads * head_rows * NY * NZ
    col = jnp.arange(group)
    per_z = n_heads * head_rows
    pick_z = (col // per_z) % NZ
    pick_y = (y_at + jnp.array(y_shift)[col // (per_z * NZ)]) % NY
    head = (col // head_rows) % n_heads
    source = head * (head_rows * NY * NZ) + (pick_y * NZ + pick_z) * head_rows + col % head_rows
    starts = [(((x_at + s) % NX) * 2 + c) * tokens for c in (core, 1 - core) for s in (2, 1, 3, 0)]
    starts = jnp.stack(starts).astype(jnp.int32)
    rows_a, rows_b, context = lax.optimization_barrier((rows_a, rows_b, context))
    ctx = arrange_context(starts, jnp.transpose(context, (1, 0, 2)), source[None, :].astype(jnp.int32))

    before_a, after_a, before_b, after_b = along_y(rows_a, 1), along_y(rows_a, -1), along_y(rows_b, 1), along_y(rows_b, -1)
    before_a, after_b = lax.optimization_barrier((before_a, after_b))
    far_a, far_b = along_y(before_a, 1), along_y(after_b, -1)
    after_a, before_b, far_a, far_b = lax.optimization_barrier((after_a, before_b, far_a, far_b))

    def blocks_of(products):
        mine, other = [[p[i * tokens : (i + 1) * tokens].astype(F32) for i in range(4)] for p in products]
        return [a + b for a, b in zip(mine, other)]

    mine_a, other_a = project(ctx, [rows_a, before_a, after_a, far_a])
    mine_b, other_b = project(ctx, [rows_b, before_b, after_b, far_b])
    other_a, other_b = other_core(other_a), other_core(other_b)
    w_in_other, w_out_other, other_b = lax.optimization_barrier((w_in_other, w_out_other, other_b))
    weights = jnp.concatenate([w_in, w_in_other], axis=1), jnp.concatenate([w_out, w_out_other])
    far_a, right_a, left_a, own_a = blocks_of((mine_a, other_a))
    far_b, right_b, left_b, own_b = blocks_of((mine_b, other_b))
    token_ids, far_a, far_b = lax.optimization_barrier((token_ids, far_a.astype(BF16), far_b.astype(BF16)))
    routes = jnp.stack([table_one[token_ids], table_two[token_ids]])
    passed_a, passed_b = along_x(far_a, 1), along_x(far_b, -1)
    left_a, right_b, routes = lax.optimization_barrier((left_a.astype(BF16), right_b.astype(BF16), routes))
    left_a, right_b = along_x(left_a, -1), along_x(right_b, 1)
    right_a = along_x((right_a + passed_a.astype(F32)).astype(BF16), 1)
    left_b = along_x((left_b + passed_b.astype(F32)).astype(BF16), -1)
    attn = [own_a + right_a.astype(F32) + left_a.astype(F32), own_b + right_b.astype(F32) + left_b.astype(F32)]
    attn = jnp.concatenate(attn, axis=1)
    state = residual.astype(F32) + attn
    scale = lax.rsqrt(jnp.mean(state * state, axis=-1, keepdims=True) + eps_norm)
    normed = (state * scale * gain).astype(BF16)

    same = routes[:, :, None] == routes[:, None, :]
    earlier = jnp.arange(tokens)[None, :] < jnp.arange(tokens)[:, None]
    rank = jnp.sum((same & earlier).astype(jnp.int32), axis=-1)
    slot = rank + CAP * jnp.arange(2)[:, None]
    main_at = jnp.where((rank < CAP) & (slot < 8), routes * 8 + slot, -1)
    rest_at = jnp.where((rank[1] < CAP) & (slot[1] >= 8), routes[1] * 8 + (slot[1] - 8) * 4, -8)
    line = jnp.arange(8 * experts)[:, None]
    to_main = (line == main_at.reshape(1, -1)).astype(BF16)
    quarter = half_width // 4
    rest_cols = jnp.concatenate([rest_at + q for q in range(4)])
    to_rest = (line == rest_cols[None, :]).astype(BF16)
    halves = jnp.concatenate([normed[:, :half_width], normed[:, half_width:]])
    quarters = jnp.concatenate(
        [normed[:, half_width + q * quarter : half_width + (q + 1) * quarter] for q in range(4)]
    )
    outgoing = jnp.concatenate([dot(to_main, halves), dot(to_rest, quarters)], axis=1).astype(BF16)

    arrived = lax.all_to_all(outgoing, "dp", split_axis=0, concat_axis=0, tiled=True)
    n = arrived.shape[0] // 2
    held = arrived[:n], arrived[n:]
    left, right, far = gather_x(*held)
    own, left, right, far = [expert_rows(h, *weights) for h in (held, left, right, far)]
    sums = scatter_x(own, right, far, left).astype(BF16)
    returned = lax.all_to_all(sums, "dp", split_axis=0, concat_axis=0, tiled=True)

    from_main = lax.dot_general(
        to_main.reshape(-1, 2, tokens), returned[:, :half_width], (((0,), (0,)), ((), ())), preferred_element_type=F32
    )
    from_rest = lax.dot_general(
        to_rest.reshape(-1, 4, tokens), returned[:, half_width:], (((0,), (0,)), ((), ())), preferred_element_type=F32
    )
    second_half = from_main[1] + jnp.concatenate([from_rest[q] for q in range(4)], axis=1)
    routed = jnp.concatenate([from_main[0], second_half], axis=1)
    return (state + routed).astype(BF16)


def solution(mesh):
    return jax.shard_map(
        on_device,
        mesh=mesh,
        in_specs=(
            P(("dp", "expert"), None),
            P("dp", "expert", None),
            P("expert", "dp", None),
            P("expert", "dp", None),
            P("expert", "dp", None),
            P("expert", "dp", None),
            P(),
            P(("dp", "expert")),
            P(),
            P(),
            P("dp", None, "expert"),
            P("dp", "expert", None),
        ),
        out_specs=P(("dp", "expert"), None),
        check_vma=False,
    )
```

```python
import jax
import jax.numpy as jnp
from jax import lax
from jax.experimental import pallas as pl
from jax.experimental.pallas import tpu as pltpu
from jax.sharding import PartitionSpec as P

lr_rate = 0.01
beta_one = 0.9
beta_two = 0.999
adam_step = 10.0
eps_adam = 1e-08
eps_norm = 1e-05

CAP = 5
NX, NY, NZ = 4, 4, 8
F32 = jnp.float32
BF16 = jnp.bfloat16


def adam_weight(master, grad, moment, second):
    new_moment = beta_one * moment + (1.0 - beta_one) * grad
    new_second = beta_two * second + (1.0 - beta_two) * grad * grad
    corr_one = 1.0 - beta_one**adam_step
    corr_two = 1.0 - beta_two**adam_step
    update = new_moment / corr_one / (jnp.sqrt(new_second / corr_two) + eps_adam)
    return (master - lr_rate * update).astype(BF16)


def along_z(x, step):
    return lax.ppermute(
        x, "dp", [(NZ * y + z, NZ * y + (z + step) % NZ) for y in range(NY) for z in range(NZ)]
    )


def along_y(x, step):
    return lax.ppermute(
        x, "dp", [(NZ * y + z, NZ * ((y + step) % NY) + z) for y in range(NY) for z in range(NZ)]
    )


def along_x(x, step):
    return lax.ppermute(x, "expert", [(i, (i + 2 * step) % (2 * NX)) for i in range(2 * NX)])


def other_core(x):
    return lax.ppermute(x, "expert", [(i, i ^ 1) for i in range(2 * NX)])


def dot(a, b):
    return jnp.dot(a, b, preferred_element_type=F32)


def add(a, b):
    return (a.astype(F32) + b.astype(F32)).astype(BF16)


def gather_x(top, bottom):
    left_top, right_bottom = along_x(top, 1), along_x(bottom, -1)
    left_bottom, right_top = along_x(bottom, 1), along_x(top, -1)
    far_top, far_bottom = along_x(left_top, 1), along_x(right_bottom, -1)
    return (left_top, left_bottom), (right_top, right_bottom), (far_top, far_bottom)


def scatter_x(own, right, far, left):
    from_left, from_right = lax.optimization_barrier((along_x(far[0], 1), along_x(far[1], -1)))
    left_bottom, right_top = along_x(right[1], 1), along_x(left[0], -1)
    left_top = along_x(add(right[0], from_left), 1)
    right_bottom = along_x(add(left[1], from_right), -1)
    top = own[0].astype(F32) + left_top.astype(F32) + right_top.astype(F32)
    bottom = own[1].astype(F32) + left_bottom.astype(F32) + right_bottom.astype(F32)
    return jnp.concatenate([top, bottom])


VMEM = pl.BlockSpec(memory_space=pltpu.VMEM)
SMEM = pl.BlockSpec(memory_space=pltpu.SMEM)


def join_kernel(*refs):
    *blocks, far_a, far_b, out_a, out_b = refs
    heads, rows, width = blocks[0].shape
    pieces = [b[h].astype(F32) for b in blocks for h in range(heads)]
    for h in range(heads):
        pieces.append(jnp.concatenate([far_a[h].astype(F32), far_b[h].astype(F32)], axis=1))
    per = 16 // rows
    for i in range(len(pieces) // per):
        sixteen = jnp.concatenate(pieces[per * i : per * (i + 1)], axis=0).astype(BF16)
        out_a[16 * i : 16 * (i + 1), :] = sixteen[:, : width // 2]
        out_b[16 * i : 16 * (i + 1), :] = sixteen[:, width // 2 :]


def join_rows(blocks, far_a, far_b):
    heads, rows, width = blocks[0].shape
    n = (len(blocks) + 1) * heads * rows
    return pl.pallas_call(
        join_kernel,
        out_shape=[jax.ShapeDtypeStruct((n, width // 2), BF16)] * 2,
        in_specs=[VMEM] * (len(blocks) + 2),
        out_specs=[VMEM] * 2,
        compiler_params=pltpu.CompilerParams(vmem_limit_bytes=12 << 20),
        cost_estimate=pl.CostEstimate(flops=0, bytes_accessed=4 * n * width, transcendentals=0),
    )(*blocks, far_a, far_b)


def context_kernel(starts, context, source, out):
    heads, _, size = context.shape
    group = source.shape[1]
    line = lax.broadcasted_iota(jnp.int32, (size, group), 0)
    order = [(line + size * h == source[...]).astype(F32).astype(BF16) for h in range(heads)]
    rows = out.shape[0] // starts.shape[0]
    for i in range(starts.shape[0]):
        at = pl.ds(pl.multiple_of(starts[i], rows), rows)
        out[rows * i : rows * (i + 1), :] = sum(dot(context[h, at, :], order[h]) for h in range(heads)).astype(BF16)


def arrange_context(starts, context, source):
    heads, tokens, size = context.shape
    return pl.pallas_call(
        context_kernel,
        out_shape=jax.ShapeDtypeStruct((tokens, heads * size), BF16),
        in_specs=[SMEM, VMEM, VMEM],
        out_specs=VMEM,
        compiler_params=pltpu.CompilerParams(vmem_limit_bytes=12 << 20),
        cost_estimate=pl.CostEstimate(
            flops=2 * tokens * heads * size * heads * size, bytes_accessed=4 * tokens * heads * size, transcendentals=0
        ),
    )(starts, context, source)


def project_kernel(ctx, *refs):
    *parts, mine, other, weight = refs
    n = parts[0].shape[0]
    for i, part in enumerate(parts):
        weight[n * i : n * (i + 1), :] = part[...]
    half = ctx.shape[0] // 2
    step = 512
    for i in range(weight.shape[1] // step):
        cols = slice(step * i, step * (i + 1))
        mine[:, cols] = dot(ctx[:half, :], weight[:, cols]).astype(BF16)
        other[:, cols] = dot(ctx[half:, :], weight[:, cols]).astype(BF16)


def project(ctx, parts):
    tokens, group = ctx.shape
    cols = parts[0].shape[1]
    return pl.pallas_call(
        project_kernel,
        out_shape=[jax.ShapeDtypeStruct((tokens // 2, cols), BF16)] * 2,
        in_specs=[VMEM] * (1 + len(parts)),
        out_specs=[VMEM] * 2,
        scratch_shapes=[pltpu.VMEM((group, cols), BF16)],
        compiler_params=pltpu.CompilerParams(vmem_limit_bytes=24 << 20),
        cost_estimate=pl.CostEstimate(
            flops=2 * tokens * group * cols, bytes_accessed=2 * (tokens * group + group * cols + tokens * cols), transcendentals=0
        ),
    )(ctx, *parts)


def expert_kernel(top, bottom, w_in, w_out, out_top, out_bottom, x, y):
    width = w_in.shape[0]
    quarter = width // 4
    n = top.shape[0]
    few = n // 4
    at = lax.broadcasted_iota(jnp.int32, (few, n), 0)
    line = lax.broadcasted_iota(jnp.int32, (few, n), 1)
    base = (at // 2) * 8 + (at % 2) * 4
    at_t = lax.broadcasted_iota(jnp.int32, (n, few), 1)
    line_t = lax.broadcasted_iota(jnp.int32, (n, few), 0)
    base_t = (at_t // 2) * 8 + (at_t % 2) * 4
    for i, half in enumerate((top, bottom)):
        x[n * i : n * (i + 1), :] = half[:, :width]
        for q in range(4):
            pick = (line == base + q).astype(F32).astype(BF16)
            x[2 * n + few * i : 2 * n + few * (i + 1), quarter * q : quarter * (q + 1)] = dot(pick, half[:, width:]).astype(BF16)
    hidden = jax.nn.gelu(dot(x[...], w_in[...]), approximate=True).astype(BF16)
    y[...] = dot(hidden, w_out[...]).astype(BF16)
    for i, half in enumerate((out_top, out_bottom)):
        half[:, :width] = y[n * i : n * (i + 1), :]
        total = 0.0
        for q in range(4):
            put = (line_t == base_t + q).astype(F32).astype(BF16)
            total += dot(put, y[2 * n + few * i : 2 * n + few * (i + 1), quarter * q : quarter * (q + 1)])
        half[:, width:] = total.astype(BF16)


def expert_rows(halves, w_in, w_out):
    n, cols = halves[0].shape
    width = w_in.shape[0]
    return pl.pallas_call(
        expert_kernel,
        out_shape=[jax.ShapeDtypeStruct((n, cols), BF16)] * 2,
        in_specs=[VMEM] * 4,
        out_specs=[VMEM] * 2,
        scratch_shapes=[pltpu.VMEM((n * 5 // 2, width), BF16)] * 2,
        compiler_params=pltpu.CompilerParams(vmem_limit_bytes=24 << 20),
        cost_estimate=pl.CostEstimate(flops=1000, bytes_accessed=1000, transcendentals=0),
    )(*halves, w_in, w_out)


def on_device(
    residual,
    context,
    master,
    grad,
    moment,
    second,
    gain,
    token_ids,
    table_one,
    table_two,
    w_in,
    w_out,
):
    tokens, width = residual.shape
    half_width = width // 2
    experts = NY * NZ
    place = lax.axis_index("expert")
    x_at, core = place // 2, place % 2
    dp_at = lax.axis_index("dp")
    y_at, z_at = dp_at // NZ, dp_at % NZ

    fresh = adam_weight(master, grad, moment, second)
    mid = width // 2
    up, down = along_z(fresh, 1), along_z(fresh, -1)
    blocks = [fresh, up, down]
    for _ in range(2):
        up, down = along_z(up, 1), along_z(down, -1)
        blocks += [up, down]
    far_a, far_b = along_z(up[..., :mid], 1), along_z(down[..., mid:], -1)
    w_in, w_out = w_in[0], w_out[0]
    w_in_other, w_out_other = other_core(w_in), other_core(w_out)
    rows_a, rows_b = join_rows(blocks, far_a, far_b)
    z_shift = [0, -1, 1, -2, 2, -3, 3, 4]
    y_shift = [0, -1, 1, 2]

    n_heads, head_rows = fresh.shape[:2]
    group = n_heads * head_rows * NY * NZ
    col = jnp.arange(group)
    per_z = n_heads * head_rows
    pick_z = (z_at + jnp.array(z_shift)[(col // per_z) % NZ]) % NZ
    pick_y = (y_at + jnp.array(y_shift)[col // (per_z * NZ)]) % NY
    head = (col // head_rows) % n_heads
    source = head * (head_rows * NY * NZ) + (pick_y * NZ + pick_z) * head_rows + col % head_rows
    starts = [(((x_at + s) % NX) * 2 + c) * tokens for c in (core, 1 - core) for s in (2, 1, 3, 0)]
    starts = jnp.stack(starts).astype(jnp.int32)
    rows_a, rows_b, context = lax.optimization_barrier((rows_a, rows_b, context))
    ctx = arrange_context(starts, jnp.transpose(context, (1, 0, 2)), source[None, :].astype(jnp.int32))

    before_a, after_a, before_b, after_b = along_y(rows_a, 1), along_y(rows_a, -1), along_y(rows_b, 1), along_y(rows_b, -1)
    before_a, after_b = lax.optimization_barrier((before_a, after_b))
    far_a, far_b = along_y(before_a, 1), along_y(after_b, -1)
    after_a, before_b, far_a, far_b, w_in_other, w_out_other = lax.optimization_barrier(
        (after_a, before_b, far_a, far_b, w_in_other, w_out_other)
    )

    def blocks_of(products):
        mine, other = [[p[i * tokens : (i + 1) * tokens].astype(F32) for i in range(4)] for p in products]
        return [a + b for a, b in zip(mine, other)]

    mine_a, other_a = project(ctx, [rows_a, before_a, after_a, far_a])
    mine_b, other_b = project(ctx, [rows_b, before_b, after_b, far_b])
    other_a, other_b = other_core(other_a), other_core(other_b)
    token_ids, other_b = lax.optimization_barrier((token_ids, other_b))
    far, right_a, left, own_a = blocks_of((mine_a, other_a))
    far, left = lax.optimization_barrier((far.astype(BF16), left.astype(BF16)))
    passed_a, left_a = along_x(far, 1), along_x(left, -1)
    far, right, left_b, own_b = blocks_of((mine_b, other_b))
    far, right = lax.optimization_barrier((far.astype(BF16), right.astype(BF16)))
    passed_b, right_b = along_x(far, -1), along_x(right, 1)
    right_a = along_x((right_a + passed_a.astype(F32)).astype(BF16), 1)
    left_b = along_x((left_b + passed_b.astype(F32)).astype(BF16), -1)
    attn = [own_a + right_a.astype(F32) + left_a.astype(F32), own_b + right_b.astype(F32) + left_b.astype(F32)]
    attn = jnp.concatenate(attn, axis=1)
    state = residual.astype(F32) + attn
    scale = lax.rsqrt(jnp.mean(state * state, axis=-1, keepdims=True) + eps_norm)
    normed = (state * scale * gain).astype(BF16)

    routes = jnp.stack([table_one[token_ids], table_two[token_ids]])
    same = routes[:, :, None] == routes[:, None, :]
    earlier = jnp.arange(tokens)[None, :] < jnp.arange(tokens)[:, None]
    rank = jnp.sum((same & earlier).astype(jnp.int32), axis=-1)
    slot = rank + CAP * jnp.arange(2)[:, None]
    main_at = jnp.where((rank < CAP) & (slot < 8), routes * 8 + slot, -1)
    rest_at = jnp.where((rank[1] < CAP) & (slot[1] >= 8), routes[1] * 8 + (slot[1] - 8) * 4, -8)
    line = jnp.arange(8 * experts)[:, None]
    to_main = (line == main_at.reshape(1, -1)).astype(BF16)
    quarter = half_width // 4
    rest_cols = jnp.concatenate([rest_at + q for q in range(4)])
    to_rest = (line == rest_cols[None, :]).astype(BF16)
    halves = jnp.concatenate([normed[:, :half_width], normed[:, half_width:]])
    quarters = jnp.concatenate(
        [normed[:, half_width + q * quarter : half_width + (q + 1) * quarter] for q in range(4)]
    )
    outgoing = jnp.concatenate([dot(to_main, halves), dot(to_rest, quarters)], axis=1).astype(BF16)

    arrived = lax.all_to_all(outgoing, "dp", split_axis=0, concat_axis=0, tiled=True)
    n = arrived.shape[0] // 2
    held = arrived[:n], arrived[n:]
    left, right, far = gather_x(*held)
    weights = jnp.concatenate([w_in, w_in_other], axis=1), jnp.concatenate([w_out, w_out_other])
    own, left, right, far = [expert_rows(h, *weights) for h in (held, left, right, far)]
    sums = scatter_x(own, right, far, left).astype(BF16)
    returned = lax.all_to_all(sums, "dp", split_axis=0, concat_axis=0, tiled=True)

    from_main = lax.dot_general(
        to_main.reshape(-1, 2, tokens), returned[:, :half_width], (((0,), (0,)), ((), ())), preferred_element_type=F32
    )
    from_rest = lax.dot_general(
        to_rest.reshape(-1, 4, tokens), returned[:, half_width:], (((0,), (0,)), ((), ())), preferred_element_type=F32
    )
    second_half = from_main[1] + jnp.concatenate([from_rest[q] for q in range(4)], axis=1)
    routed = jnp.concatenate([from_main[0], second_half], axis=1)
    return (state + routed).astype(BF16)


def solution(mesh):
    return jax.shard_map(
        on_device,
        mesh=mesh,
        in_specs=(
            P(("dp", "expert"), None),
            P("dp", "expert", None),
            P("expert", "dp", None),
            P("expert", "dp", None),
            P("expert", "dp", None),
            P("expert", "dp", None),
            P(),
            P(("dp", "expert")),
            P(),
            P(),
            P("dp", None, "expert"),
            P("dp", "expert", None),
        ),
        out_specs=P(("dp", "expert"), None),
        check_vma=False,
    )
```

```python
import jax
import jax.numpy as jnp
from jax import lax
from jax.experimental import pallas as pl
from jax.experimental.pallas import tpu as pltpu
from jax.sharding import PartitionSpec as P

lr_rate = 0.01
beta_one = 0.9
beta_two = 0.999
adam_step = 10.0
eps_adam = 1e-08
eps_norm = 1e-05

CAP = 5
NX, NY, NZ = 4, 4, 8
F32 = jnp.float32
BF16 = jnp.bfloat16


def adam_weight(master, grad, moment, second):
    new_moment = beta_one * moment + (1.0 - beta_one) * grad
    new_second = beta_two * second + (1.0 - beta_two) * grad * grad
    corr_one = 1.0 - beta_one**adam_step
    corr_two = 1.0 - beta_two**adam_step
    update = new_moment / corr_one / (jnp.sqrt(new_second / corr_two) + eps_adam)
    return (master - lr_rate * update).astype(BF16)


def along_z(x, step):
    return lax.ppermute(
        x, "dp", [(NZ * y + z, NZ * y + (z + step) % NZ) for y in range(NY) for z in range(NZ)]
    )


def along_y(x, step):
    return lax.ppermute(
        x, "dp", [(NZ * y + z, NZ * ((y + step) % NY) + z) for y in range(NY) for z in range(NZ)]
    )


def along_x(x, step):
    return lax.ppermute(x, "expert", [(i, (i + 2 * step) % (2 * NX)) for i in range(2 * NX)])


def other_core(x):
    return lax.ppermute(x, "expert", [(i, i ^ 1) for i in range(2 * NX)])


def dot(a, b):
    return jnp.dot(a, b, preferred_element_type=F32)


def add(a, b):
    return (a.astype(F32) + b.astype(F32)).astype(BF16)


def gather_x(top, bottom):
    left_top, right_bottom = along_x(top, 1), along_x(bottom, -1)
    left_bottom, right_top = along_x(bottom, 1), along_x(top, -1)
    far_top, far_bottom = along_x(left_top, 1), along_x(right_bottom, -1)
    return (left_top, left_bottom), (right_top, right_bottom), (far_top, far_bottom)


def scatter_x(own, right, far, left):
    from_left, from_right = lax.optimization_barrier((along_x(far[0], 1), along_x(far[1], -1)))
    left_bottom, right_top = along_x(right[1], 1), along_x(left[0], -1)
    left_top = along_x(add(right[0], from_left), 1)
    right_bottom = along_x(add(left[1], from_right), -1)
    top = own[0].astype(F32) + left_top.astype(F32) + right_top.astype(F32)
    bottom = own[1].astype(F32) + left_bottom.astype(F32) + right_bottom.astype(F32)
    return jnp.concatenate([top, bottom])


VMEM = pl.BlockSpec(memory_space=pltpu.VMEM)
SMEM = pl.BlockSpec(memory_space=pltpu.SMEM)


def join_kernel(*refs):
    *blocks, far_a, far_b, out_a, out_b = refs
    heads, rows, width = blocks[0].shape
    pieces = [b[h].astype(F32) for b in blocks for h in range(heads)]
    for h in range(heads):
        pieces.append(jnp.concatenate([far_a[h].astype(F32), far_b[h].astype(F32)], axis=1))
    per = 16 // rows
    for i in range(len(pieces) // per):
        sixteen = jnp.concatenate(pieces[per * i : per * (i + 1)], axis=0).astype(BF16)
        out_a[16 * i : 16 * (i + 1), :] = sixteen[:, : width // 2]
        out_b[16 * i : 16 * (i + 1), :] = sixteen[:, width // 2 :]


def join_rows(blocks, far_a, far_b):
    heads, rows, width = blocks[0].shape
    n = (len(blocks) + 1) * heads * rows
    return pl.pallas_call(
        join_kernel,
        out_shape=[jax.ShapeDtypeStruct((n, width // 2), BF16)] * 2,
        in_specs=[VMEM] * (len(blocks) + 2),
        out_specs=[VMEM] * 2,
        compiler_params=pltpu.CompilerParams(vmem_limit_bytes=16 << 20),
        cost_estimate=pl.CostEstimate(flops=0, bytes_accessed=4 * n * width, transcendentals=0),
    )(*blocks, far_a, far_b)


def context_kernel(starts, context, source, out):
    heads, _, size = context.shape
    group = source.shape[1]
    line = lax.broadcasted_iota(jnp.int32, (size, group), 0)
    order = [(line + size * h == source[...]).astype(F32).astype(BF16) for h in range(heads)]
    rows = out.shape[0] // starts.shape[0]
    for i in range(starts.shape[0]):
        at = pl.ds(pl.multiple_of(starts[i], rows), rows)
        out[rows * i : rows * (i + 1), :] = sum(dot(context[h, at, :], order[h]) for h in range(heads)).astype(BF16)


def arrange_context(starts, context, source):
    heads, tokens, size = context.shape
    return pl.pallas_call(
        context_kernel,
        out_shape=jax.ShapeDtypeStruct((tokens, heads * size), BF16),
        in_specs=[SMEM, VMEM, VMEM],
        out_specs=VMEM,
        compiler_params=pltpu.CompilerParams(vmem_limit_bytes=16 << 20),
        cost_estimate=pl.CostEstimate(
            flops=2 * tokens * heads * size * heads * size, bytes_accessed=4 * tokens * heads * size, transcendentals=0
        ),
    )(starts, context, source)


def project_kernel(ctx, *refs):
    *parts, mine, other, weight = refs
    n = parts[0].shape[0]
    for i, part in enumerate(parts):
        weight[n * i : n * (i + 1), :] = part[...]
    half = ctx.shape[0] // 2
    step = 512
    for i in range(weight.shape[1] // step):
        cols = slice(step * i, step * (i + 1))
        mine[:, cols] = dot(ctx[:half, :], weight[:, cols]).astype(BF16)
        other[:, cols] = dot(ctx[half:, :], weight[:, cols]).astype(BF16)


def project(ctx, parts):
    tokens, group = ctx.shape
    cols = parts[0].shape[1]
    return pl.pallas_call(
        project_kernel,
        out_shape=[jax.ShapeDtypeStruct((tokens // 2, cols), BF16)] * 2,
        in_specs=[VMEM] * (1 + len(parts)),
        out_specs=[VMEM] * 2,
        scratch_shapes=[pltpu.VMEM((group, cols), BF16)],
        compiler_params=pltpu.CompilerParams(vmem_limit_bytes=24 << 20),
        cost_estimate=pl.CostEstimate(
            flops=2 * tokens * group * cols, bytes_accessed=2 * (tokens * group + group * cols + tokens * cols), transcendentals=0
        ),
    )(ctx, *parts)


def expert_kernel(top, bottom, w_in, w_out, out_top, out_bottom, x, y):
    width = w_in.shape[0]
    quarter = width // 4
    n = top.shape[0]
    few = n // 4
    at = lax.broadcasted_iota(jnp.int32, (few, n), 0)
    line = lax.broadcasted_iota(jnp.int32, (few, n), 1)
    base = (at // 2) * 8 + (at % 2) * 4
    at_t = lax.broadcasted_iota(jnp.int32, (n, few), 1)
    line_t = lax.broadcasted_iota(jnp.int32, (n, few), 0)
    base_t = (at_t // 2) * 8 + (at_t % 2) * 4
    for i, half in enumerate((top, bottom)):
        x[n * i : n * (i + 1), :] = half[:, :width]
        for q in range(4):
            pick = (line == base + q).astype(F32).astype(BF16)
            x[2 * n + few * i : 2 * n + few * (i + 1), quarter * q : quarter * (q + 1)] = dot(pick, half[:, width:]).astype(BF16)
    hidden = jax.nn.gelu(dot(x[...], w_in[...]), approximate=True).astype(BF16)
    y[...] = dot(hidden, w_out[...]).astype(BF16)
    for i, half in enumerate((out_top, out_bottom)):
        half[:, :width] = y[n * i : n * (i + 1), :]
        total = 0.0
        for q in range(4):
            put = (line_t == base_t + q).astype(F32).astype(BF16)
            total += dot(put, y[2 * n + few * i : 2 * n + few * (i + 1), quarter * q : quarter * (q + 1)])
        half[:, width:] = total.astype(BF16)


def expert_rows(halves, w_in, w_out):
    n, cols = halves[0].shape
    width = w_in.shape[0]
    return pl.pallas_call(
        expert_kernel,
        out_shape=[jax.ShapeDtypeStruct((n, cols), BF16)] * 2,
        in_specs=[VMEM] * 4,
        out_specs=[VMEM] * 2,
        scratch_shapes=[pltpu.VMEM((n * 5 // 2, width), BF16)] * 2,
        compiler_params=pltpu.CompilerParams(vmem_limit_bytes=24 << 20),
        cost_estimate=pl.CostEstimate(flops=1000, bytes_accessed=1000, transcendentals=0),
    )(*halves, w_in, w_out)


def on_device(
    residual,
    context,
    master,
    grad,
    moment,
    second,
    gain,
    token_ids,
    table_one,
    table_two,
    w_in,
    w_out,
):
    tokens, width = residual.shape
    half_width = width // 2
    experts = NY * NZ
    place = lax.axis_index("expert")
    x_at, core = place // 2, place % 2
    dp_at = lax.axis_index("dp")
    y_at, z_at = dp_at // NZ, dp_at % NZ

    fresh = adam_weight(master, grad, moment, second)
    mid = width // 2
    up, down = along_z(fresh, 1), along_z(fresh, -1)
    blocks = [fresh, up, down]
    for _ in range(2):
        up, down = along_z(up, 1), along_z(down, -1)
        blocks += [up, down]
    far_a, far_b = along_z(up[..., :mid], 1), along_z(down[..., mid:], -1)
    w_in, w_out = w_in[0], w_out[0]
    w_in_other, w_out_other = other_core(w_in), other_core(w_out)
    far_a, w_in_other, w_out_other = lax.optimization_barrier((far_a, w_in_other, w_out_other))
    rows_a, rows_b = join_rows(blocks, far_a, far_b)
    z_shift = [0, -1, 1, -2, 2, -3, 3, 4]
    y_shift = [0, -1, 1, 2]

    n_heads, head_rows = fresh.shape[:2]
    group = n_heads * head_rows * NY * NZ
    col = jnp.arange(group)
    per_z = n_heads * head_rows
    pick_z = (z_at + jnp.array(z_shift)[(col // per_z) % NZ]) % NZ
    pick_y = (y_at + jnp.array(y_shift)[col // (per_z * NZ)]) % NY
    head = (col // head_rows) % n_heads
    source = head * (head_rows * NY * NZ) + (pick_y * NZ + pick_z) * head_rows + col % head_rows
    starts = [(((x_at + s) % NX) * 2 + c) * tokens for c in (core, 1 - core) for s in (2, 1, 3, 0)]
    starts = jnp.stack(starts).astype(jnp.int32)
    rows_a, rows_b, context = lax.optimization_barrier((rows_a, rows_b, context))
    ctx = arrange_context(starts, jnp.transpose(context, (1, 0, 2)), source[None, :].astype(jnp.int32))

    attn = []
    for rows, way in ((rows_a, 1), (rows_b, -1)):
        before, after = along_y(rows, 1), along_y(rows, -1)
        far = along_y(before if way == 1 else after, way)
        mine, other = project(ctx, [rows, before, after, far])
        other = other_core(other)
        far, right, left, own = [
            mine[i * tokens : (i + 1) * tokens].astype(F32) + other[i * tokens : (i + 1) * tokens].astype(F32) for i in range(4)
        ]
        passed = along_x(far.astype(BF16), way).astype(F32)
        right, left = (right + passed, left) if way == 1 else (right, left + passed)
        attn.append(own + along_x(right.astype(BF16), 1).astype(F32) + along_x(left.astype(BF16), -1).astype(F32))
    attn = jnp.concatenate(attn, axis=1)
    state = residual.astype(F32) + attn
    scale = lax.rsqrt(jnp.mean(state * state, axis=-1, keepdims=True) + eps_norm)
    normed = (state * scale * gain).astype(BF16)

    routes = jnp.stack([table_one[token_ids], table_two[token_ids]])
    same = routes[:, :, None] == routes[:, None, :]
    earlier = jnp.arange(tokens)[None, :] < jnp.arange(tokens)[:, None]
    rank = jnp.sum((same & earlier).astype(jnp.int32), axis=-1)
    slot = rank + CAP * jnp.arange(2)[:, None]
    main_at = jnp.where((rank < CAP) & (slot < 8), routes * 8 + slot, -1)
    rest_at = jnp.where((rank[1] < CAP) & (slot[1] >= 8), routes[1] * 8 + (slot[1] - 8) * 4, -8)
    line = jnp.arange(8 * experts)[:, None]
    to_main = (line == main_at.reshape(1, -1)).astype(BF16)
    quarter = half_width // 4
    rest_cols = jnp.concatenate([rest_at + q for q in range(4)])
    to_rest = (line == rest_cols[None, :]).astype(BF16)
    halves = jnp.concatenate([normed[:, :half_width], normed[:, half_width:]])
    quarters = jnp.concatenate(
        [normed[:, half_width + q * quarter : half_width + (q + 1) * quarter] for q in range(4)]
    )
    outgoing = jnp.concatenate([dot(to_main, halves), dot(to_rest, quarters)], axis=1).astype(BF16)

    arrived = lax.all_to_all(outgoing, "dp", split_axis=0, concat_axis=0, tiled=True)
    n = arrived.shape[0] // 2
    held = arrived[:n], arrived[n:]
    left, right, far = gather_x(*held)
    weights = jnp.concatenate([w_in, w_in_other], axis=1), jnp.concatenate([w_out, w_out_other])
    own = expert_rows(held, *weights)
    far, own = lax.optimization_barrier((far, own))
    far, right, left = [expert_rows(h, *weights) for h in (far, right, left)]
    sums = scatter_x(own, right, far, left).astype(BF16)
    returned = lax.all_to_all(sums, "dp", split_axis=0, concat_axis=0, tiled=True)

    from_main = lax.dot_general(
        to_main.reshape(-1, 2, tokens), returned[:, :half_width], (((0,), (0,)), ((), ())), preferred_element_type=F32
    )
    from_rest = lax.dot_general(
        to_rest.reshape(-1, 4, tokens), returned[:, half_width:], (((0,), (0,)), ((), ())), preferred_element_type=F32
    )
    second_half = from_main[1] + jnp.concatenate([from_rest[q] for q in range(4)], axis=1)
    routed = jnp.concatenate([from_main[0], second_half], axis=1)
    return (state + routed).astype(BF16)


def solution(mesh):
    return jax.shard_map(
        on_device,
        mesh=mesh,
        in_specs=(
            P(("dp", "expert"), None),
            P("dp", "expert", None),
            P("expert", "dp", None),
            P("expert", "dp", None),
            P("expert", "dp", None),
            P("expert", "dp", None),
            P(),
            P(("dp", "expert")),
            P(),
            P(),
            P("dp", None, "expert"),
            P("dp", "expert", None),
        ),
        out_specs=P(("dp", "expert"), None),
        check_vma=False,
    )
```

```python
import jax
import jax.numpy as jnp
from jax import lax
from jax.experimental import pallas as pl
from jax.experimental.pallas import tpu as pltpu
from jax.sharding import PartitionSpec as P

lr_rate = 0.01
beta_one = 0.9
beta_two = 0.999
adam_step = 10.0
eps_adam = 1e-08
eps_norm = 1e-05

CAP = 5
NX, NY, NZ = 4, 4, 8
F32 = jnp.float32
BF16 = jnp.bfloat16


def adam_weight(master, grad, moment, second):
    new_moment = beta_one * moment + (1.0 - beta_one) * grad
    new_second = beta_two * second + (1.0 - beta_two) * grad * grad
    corr_one = 1.0 - beta_one**adam_step
    corr_two = 1.0 - beta_two**adam_step
    update = new_moment / corr_one / (jnp.sqrt(new_second / corr_two) + eps_adam)
    return (master - lr_rate * update).astype(BF16)


def along_z(x, step):
    return lax.ppermute(
        x, "dp", [(NZ * y + z, NZ * y + (z + step) % NZ) for y in range(NY) for z in range(NZ)]
    )


def along_y(x, step):
    return lax.ppermute(
        x, "dp", [(NZ * y + z, NZ * ((y + step) % NY) + z) for y in range(NY) for z in range(NZ)]
    )


def along_x(x, step):
    return lax.ppermute(x, "expert", [(i, (i + 2 * step) % (2 * NX)) for i in range(2 * NX)])


def other_core(x):
    return lax.ppermute(x, "expert", [(i, i ^ 1) for i in range(2 * NX)])


def dot(a, b):
    return jnp.dot(a, b, preferred_element_type=F32)


def add(a, b):
    return (a.astype(F32) + b.astype(F32)).astype(BF16)


def gather_x(top, bottom):
    left_top, right_bottom = along_x(top, 1), along_x(bottom, -1)
    left_bottom, right_top = along_x(bottom, 1), along_x(top, -1)
    far_top, far_bottom = along_x(left_top, 1), along_x(right_bottom, -1)
    return (left_top, left_bottom), (right_top, right_bottom), (far_top, far_bottom)


def scatter_x(own, right, far, left):
    from_left, from_right = lax.optimization_barrier((along_x(far[0], 1), along_x(far[1], -1)))
    left_bottom, right_top = along_x(right[1], 1), along_x(left[0], -1)
    left_top = along_x(add(right[0], from_left), 1)
    right_bottom = along_x(add(left[1], from_right), -1)
    top = own[0].astype(F32) + left_top.astype(F32) + right_top.astype(F32)
    bottom = own[1].astype(F32) + left_bottom.astype(F32) + right_bottom.astype(F32)
    return jnp.concatenate([top, bottom])


VMEM = pl.BlockSpec(memory_space=pltpu.VMEM)
SMEM = pl.BlockSpec(memory_space=pltpu.SMEM)


def join_kernel(*refs):
    *blocks, far_a, far_b, out_a, out_b = refs
    heads, rows, width = blocks[0].shape
    pieces = [b[h].astype(F32) for b in blocks for h in range(heads)]
    for h in range(heads):
        pieces.append(jnp.concatenate([far_a[h].astype(F32), far_b[h].astype(F32)], axis=1))
    per = 16 // rows
    for i in range(len(pieces) // per):
        sixteen = jnp.concatenate(pieces[per * i : per * (i + 1)], axis=0).astype(BF16)
        out_a[16 * i : 16 * (i + 1), :] = sixteen[:, : width // 2]
        out_b[16 * i : 16 * (i + 1), :] = sixteen[:, width // 2 :]


def join_rows(blocks, far_a, far_b):
    heads, rows, width = blocks[0].shape
    n = (len(blocks) + 1) * heads * rows
    return pl.pallas_call(
        join_kernel,
        out_shape=[jax.ShapeDtypeStruct((n, width // 2), BF16)] * 2,
        in_specs=[VMEM] * (len(blocks) + 2),
        out_specs=[VMEM] * 2,
        compiler_params=pltpu.CompilerParams(vmem_limit_bytes=16 << 20),
        cost_estimate=pl.CostEstimate(flops=0, bytes_accessed=4 * n * width, transcendentals=0),
    )(*blocks, far_a, far_b)


def context_kernel(starts, context, source, out):
    heads, _, size = context.shape
    group = source.shape[1]
    line = lax.broadcasted_iota(jnp.int32, (size, group), 0)
    order = [(line + size * h == source[...]).astype(F32).astype(BF16) for h in range(heads)]
    rows = out.shape[0] // starts.shape[0]
    for i in range(starts.shape[0]):
        at = pl.ds(pl.multiple_of(starts[i], rows), rows)
        out[rows * i : rows * (i + 1), :] = sum(dot(context[h, at, :], order[h]) for h in range(heads)).astype(BF16)


def arrange_context(starts, context, source):
    heads, tokens, size = context.shape
    return pl.pallas_call(
        context_kernel,
        out_shape=jax.ShapeDtypeStruct((tokens, heads * size), BF16),
        in_specs=[SMEM, VMEM, VMEM],
        out_specs=VMEM,
        compiler_params=pltpu.CompilerParams(vmem_limit_bytes=16 << 20),
        cost_estimate=pl.CostEstimate(
            flops=2 * tokens * heads * size * heads * size, bytes_accessed=4 * tokens * heads * size, transcendentals=0
        ),
    )(starts, context, source)


def project_kernel(ctx, *refs):
    *parts, mine, other, weight = refs
    n = parts[0].shape[0]
    for i, part in enumerate(parts):
        weight[n * i : n * (i + 1), :] = part[...]
    half = ctx.shape[0] // 2
    step = 512
    for i in range(weight.shape[1] // step):
        cols = slice(step * i, step * (i + 1))
        mine[:, cols] = dot(ctx[:half, :], weight[:, cols]).astype(BF16)
        other[:, cols] = dot(ctx[half:, :], weight[:, cols]).astype(BF16)


def project(ctx, parts):
    tokens, group = ctx.shape
    cols = parts[0].shape[1]
    return pl.pallas_call(
        project_kernel,
        out_shape=[jax.ShapeDtypeStruct((tokens // 2, cols), BF16)] * 2,
        in_specs=[VMEM] * (1 + len(parts)),
        out_specs=[VMEM] * 2,
        scratch_shapes=[pltpu.VMEM((group, cols), BF16)],
        compiler_params=pltpu.CompilerParams(vmem_limit_bytes=24 << 20),
        cost_estimate=pl.CostEstimate(
            flops=2 * tokens * group * cols, bytes_accessed=2 * (tokens * group + group * cols + tokens * cols), transcendentals=0
        ),
    )(ctx, *parts)


def expert_kernel(top, bottom, w_in, w_out, out_top, out_bottom, x, y):
    width = w_in.shape[0]
    quarter = width // 4
    n = top.shape[0]
    few = n // 4
    at = lax.broadcasted_iota(jnp.int32, (few, n), 0)
    line = lax.broadcasted_iota(jnp.int32, (few, n), 1)
    base = (at // 2) * 8 + (at % 2) * 4
    at_t = lax.broadcasted_iota(jnp.int32, (n, few), 1)
    line_t = lax.broadcasted_iota(jnp.int32, (n, few), 0)
    base_t = (at_t // 2) * 8 + (at_t % 2) * 4
    for i, half in enumerate((top, bottom)):
        x[n * i : n * (i + 1), :] = half[:, :width]
        for q in range(4):
            pick = (line == base + q).astype(F32).astype(BF16)
            x[2 * n + few * i : 2 * n + few * (i + 1), quarter * q : quarter * (q + 1)] = dot(pick, half[:, width:]).astype(BF16)
    hidden = jax.nn.gelu(dot(x[...], w_in[...]), approximate=True).astype(BF16)
    y[...] = dot(hidden, w_out[...]).astype(BF16)
    for i, half in enumerate((out_top, out_bottom)):
        half[:, :width] = y[n * i : n * (i + 1), :]
        total = 0.0
        for q in range(4):
            put = (line_t == base_t + q).astype(F32).astype(BF16)
            total += dot(put, y[2 * n + few * i : 2 * n + few * (i + 1), quarter * q : quarter * (q + 1)])
        half[:, width:] = total.astype(BF16)


def expert_rows(halves, w_in, w_out):
    n, cols = halves[0].shape
    width = w_in.shape[0]
    return pl.pallas_call(
        expert_kernel,
        out_shape=[jax.ShapeDtypeStruct((n, cols), BF16)] * 2,
        in_specs=[VMEM] * 4,
        out_specs=[VMEM] * 2,
        scratch_shapes=[pltpu.VMEM((n * 5 // 2, width), BF16)] * 2,
        compiler_params=pltpu.CompilerParams(vmem_limit_bytes=24 << 20),
        cost_estimate=pl.CostEstimate(flops=1000, bytes_accessed=1000, transcendentals=0),
    )(*halves, w_in, w_out)


def on_device(
    residual,
    context,
    master,
    grad,
    moment,
    second,
    gain,
    token_ids,
    table_one,
    table_two,
    w_in,
    w_out,
):
    tokens, width = residual.shape
    half_width = width // 2
    experts = NY * NZ
    place = lax.axis_index("expert")
    x_at, core = place // 2, place % 2
    dp_at = lax.axis_index("dp")
    y_at, z_at = dp_at // NZ, dp_at % NZ

    fresh = adam_weight(master, grad, moment, second)
    mid = width // 2
    up, down = along_z(fresh, 1), along_z(fresh, -1)
    blocks = [fresh, up, down]
    for _ in range(2):
        up, down = along_z(up, 1), along_z(down, -1)
        blocks += [up, down]
    far_a, far_b = along_z(up[..., :mid], 1), along_z(down[..., mid:], -1)
    w_in, w_out = w_in[0], w_out[0]
    w_in_other, w_out_other = other_core(w_in), other_core(w_out)
    rows_a, rows_b = join_rows(blocks, far_a, far_b)
    z_shift = [0, -1, 1, -2, 2, -3, 3, 4]
    y_shift = [0, -1, 1, 2]

    n_heads, head_rows = fresh.shape[:2]
    group = n_heads * head_rows * NY * NZ
    col = jnp.arange(group)
    per_z = n_heads * head_rows
    pick_z = (z_at + jnp.array(z_shift)[(col // per_z) % NZ]) % NZ
    pick_y = (y_at + jnp.array(y_shift)[col // (per_z * NZ)]) % NY
    head = (col // head_rows) % n_heads
    source = head * (head_rows * NY * NZ) + (pick_y * NZ + pick_z) * head_rows + col % head_rows
    starts = [(((x_at + s) % NX) * 2 + c) * tokens for c in (core, 1 - core) for s in (2, 1, 3, 0)]
    starts = jnp.stack(starts).astype(jnp.int32)
    rows_a, rows_b, context = lax.optimization_barrier((rows_a, rows_b, context))
    ctx = arrange_context(starts, jnp.transpose(context, (1, 0, 2)), source[None, :].astype(jnp.int32))
    ctx, w_in_other, w_out_other = lax.optimization_barrier((ctx, w_in_other, w_out_other))

    attn = []
    for rows, way in ((rows_a, 1), (rows_b, -1)):
        before, after = along_y(rows, 1), along_y(rows, -1)
        far = along_y(before if way == 1 else after, way)
        mine, other = project(ctx, [rows, before, after, far])
        other = other_core(other)
        far, right, left, own = [
            mine[i * tokens : (i + 1) * tokens].astype(F32) + other[i * tokens : (i + 1) * tokens].astype(F32) for i in range(4)
        ]
        passed = along_x(far.astype(BF16), way).astype(F32)
        right, left = (right + passed, left) if way == 1 else (right, left + passed)
        attn.append(own + along_x(right.astype(BF16), 1).astype(F32) + along_x(left.astype(BF16), -1).astype(F32))
    attn = jnp.concatenate(attn, axis=1)
    state = residual.astype(F32) + attn
    scale = lax.rsqrt(jnp.mean(state * state, axis=-1, keepdims=True) + eps_norm)
    normed = (state * scale * gain).astype(BF16)

    routes = jnp.stack([table_one[token_ids], table_two[token_ids]])
    same = routes[:, :, None] == routes[:, None, :]
    earlier = jnp.arange(tokens)[None, :] < jnp.arange(tokens)[:, None]
    rank = jnp.sum((same & earlier).astype(jnp.int32), axis=-1)
    slot = rank + CAP * jnp.arange(2)[:, None]
    main_at = jnp.where((rank < CAP) & (slot < 8), routes * 8 + slot, -1)
    rest_at = jnp.where((rank[1] < CAP) & (slot[1] >= 8), routes[1] * 8 + (slot[1] - 8) * 4, -8)
    line = jnp.arange(8 * experts)[:, None]
    to_main = (line == main_at.reshape(1, -1)).astype(BF16)
    quarter = half_width // 4
    rest_cols = jnp.concatenate([rest_at + q for q in range(4)])
    to_rest = (line == rest_cols[None, :]).astype(BF16)
    halves = jnp.concatenate([normed[:, :half_width], normed[:, half_width:]])
    quarters = jnp.concatenate(
        [normed[:, half_width + q * quarter : half_width + (q + 1) * quarter] for q in range(4)]
    )
    outgoing = jnp.concatenate([dot(to_main, halves), dot(to_rest, quarters)], axis=1).astype(BF16)

    arrived = lax.all_to_all(outgoing, "dp", split_axis=0, concat_axis=0, tiled=True)
    n = arrived.shape[0] // 2
    held = arrived[:n], arrived[n:]
    left, right, far = gather_x(*held)
    weights = jnp.concatenate([w_in, w_in_other], axis=1), jnp.concatenate([w_out, w_out_other])
    own = expert_rows(held, *weights)
    far, own = lax.optimization_barrier((far, own))
    far, right, left = [expert_rows(h, *weights) for h in (far, right, left)]
    sums = scatter_x(own, right, far, left).astype(BF16)
    returned = lax.all_to_all(sums, "dp", split_axis=0, concat_axis=0, tiled=True)

    from_main = lax.dot_general(
        to_main.reshape(-1, 2, tokens), returned[:, :half_width], (((0,), (0,)), ((), ())), preferred_element_type=F32
    )
    from_rest = lax.dot_general(
        to_rest.reshape(-1, 4, tokens), returned[:, half_width:], (((0,), (0,)), ((), ())), preferred_element_type=F32
    )
    second_half = from_main[1] + jnp.concatenate([from_rest[q] for q in range(4)], axis=1)
    routed = jnp.concatenate([from_main[0], second_half], axis=1)
    return (state + routed).astype(BF16)


def solution(mesh):
    return jax.shard_map(
        on_device,
        mesh=mesh,
        in_specs=(
            P(("dp", "expert"), None),
            P("dp", "expert", None),
            P("expert", "dp", None),
            P("expert", "dp", None),
            P("expert", "dp", None),
            P("expert", "dp", None),
            P(),
            P(("dp", "expert")),
            P(),
            P(),
            P("dp", None, "expert"),
            P("dp", "expert", None),
        ),
        out_specs=P(("dp", "expert"), None),
        check_vma=False,
    )
```
